768 devices in a mesh: ctx: 64 (over y, x, core), head: 12 (over z).
Axes of the slice: x: 4, y: 8, z: 12, core: 2. Of those that a mesh axis runs over, the one named last changes fastest.
Arguments:
- query_lin: bfloat16 [32768, 1536], P('ctx', 'head'), may hold values from -6 to 6
- key_lin: bfloat16 [32768, 1536], P('ctx', 'head'), may hold values from -6 to 6
- value_lin: bfloat16 [32768, 1536], P('ctx', 'head'), may hold values from -6 to 6
- norm_gain: float32 [1536], P('head'), may hold values from 0.5 to 2
- grad_normed: bfloat16 [32768, 1536], P('ctx', 'head'), may hold values from -6 to 6
- query_win: bfloat16 [32768, 1536], P('ctx', 'head'), may hold values from -5 to 5
- key_win: bfloat16 [32768, 1536], P('ctx', 'head'), may hold values from -5 to 5
- value_win: bfloat16 [32768, 1536], P('ctx', 'head'), may hold values from -6 to 6
- grad_win: bfloat16 [32768, 1536], P('ctx', 'head'), may hold values from -6 to 6
Outputs:
- grad_query_lin: bfloat16 [32768, 1536], P('ctx', 'head')
- grad_key_lin: bfloat16 [32768, 1536], P('ctx', 'head')
- grad_value_lin: bfloat16 [32768, 1536], P('ctx', 'head')
- grad_query_win: bfloat16 [32768, 1536], P('ctx', 'head')
- grad_key_win: bfloat16 [32768, 1536], P('ctx', 'head')
- grad_value_win: bfloat16 [32768, 1536], P('ctx', 'head')
The draws below stay inside these ranges and needn't reach their ends.
All inputs are finite; a program needn't handle non-finite values.
Results may differ from the reference program's by a relative error of at most 0.012.
Values may be sent and summed in bfloat16 or wider, within the bound.
No kernel may reach another device: no remote copies, remote signals or barrier semaphores. Data moves between devices by JAX's collectives and lax.ppermute only.
A program may use at most 32 MiB of HBM per device.

```python
import math
import jax
import jax.numpy as jnp
from jax import lax

DH = 128
HEADS = 12
WIDTH = 1536
GROUP = 512
WINDOW = 512
TOKENS = 32768


def window_pair(key):
    base = jax.random.fold_in(key, 7)
    first, second = jax.random.split(base, 2)
    shape = (TOKENS, HEADS * DH)
    queries = jnp.clip(jax.random.normal(first, shape, jnp.float32), -5.0, 5.0)
    keyset = jnp.clip(jax.random.normal(second, shape, jnp.float32), -5.0, 5.0)
    return (queries, keyset)


def draw_query_win(key, part):
    return window_pair(key)[0].astype(jnp.bfloat16)


def draw_key_win(key, part):
    return window_pair(key)[1].astype(jnp.bfloat16)


def level_of(key, dims, cuts, least, largest):
    gain, own = 1.0, jax.random.fold_in(key, 6)
    for position, blocks in cuts:
        draws = jnp.exp(jax.random.uniform(jax.random.fold_in(own, position), (blocks,), jnp.float32, least / len(cuts), largest / len(cuts)))
        gain = gain * jnp.repeat(draws, dims[position] // blocks).reshape([-1 if axis == position else 1 for axis in range(len(dims))])
    return gain


def scatter_about(key, extent, scale, most, cuts=(), held_as=jnp.bfloat16):
    factor_of = level_of(key, extent, cuts, -0.22, 0.18) if cuts else 1.0
    entries = jax.random.normal(key, extent, jnp.float32) * scale * factor_of
    return jnp.minimum(jnp.maximum(entries, -most), most).astype(held_as)


def setup_inputs(seed: int = 0) -> dict:
    key_list = jax.random.split(jax.random.key(seed), 10)
    query_lin = scatter_about(key_list[0], (TOKENS, WIDTH), 1.0, 6.0, ((0, 64), (1, 12)))
    key_lin = scatter_about(key_list[1], (TOKENS, WIDTH), 1.0, 6.0, ((0, 64), (1, 12)))
    value_lin = scatter_about(key_list[2], (TOKENS, WIDTH), 1.0, 6.0, ((0, 64), (1, 12)))
    norm_gain = jnp.clip(jnp.exp(math.log(2.0) - 1.3862944 * jax.random.uniform(key_list[3], (WIDTH,), jnp.float32) ** level_of(key_list[3], (WIDTH,), ((0, 12),), -0.2, 0.2)), 0.5, 2.0)
    grad_normed = scatter_about(key_list[4], (TOKENS, WIDTH), 1.0, 6.0, ((0, 64), (1, 12)))
    query_win = draw_query_win(jax.random.fold_in(key_list[9], 71), 0)
    key_win = draw_key_win(jax.random.fold_in(key_list[9], 71), 0)
    value_win = scatter_about(key_list[7], (TOKENS, WIDTH), 1.0, 6.0, ((0, 64), (1, 12)))
    grad_win = scatter_about(key_list[8], (TOKENS, WIDTH), 1.0, 6.0, ((0, 64), (1, 12)))
    return dict(query_lin=query_lin, key_lin=key_lin, value_lin=value_lin, norm_gain=norm_gain, grad_normed=grad_normed, query_win=query_win, key_win=key_win, value_win=value_win, grad_win=grad_win)


norm_eps = 1e-06
highest = lax.Precision.HIGHEST

def rounded(values):
    return lax.optimization_barrier(values.astype(jnp.bfloat16)).astype(jnp.float32)

def settle(extended):
    own = extended[:, WINDOW:]
    following = jnp.concatenate([extended[1:, :WINDOW], jnp.zeros_like(extended[:1, :WINDOW])], 0)
    own = own.at[:, GROUP - WINDOW:].add(following)
    return own.reshape(TOKENS, WIDTH).astype(jnp.bfloat16)

def reference(query_lin, key_lin, value_lin, norm_gain, grad_normed, query_win, key_win, value_win, grad_win):
    blocks = TOKENS // GROUP
    shaped = (blocks, GROUP, HEADS, DH)
    queries = query_lin.astype(jnp.float32).reshape(shaped)
    keys_lin = key_lin.astype(jnp.float32).reshape(shaped)
    values_lin = value_lin.astype(jnp.float32).reshape(shaped)
    local_state = jnp.einsum('ntha,nthb->nhab', keys_lin, values_lin)
    running = jnp.cumsum(local_state, 0)
    prior = jnp.concatenate([jnp.zeros_like(local_state[:1]), running[:-1]], 0)
    lower = jnp.arange(GROUP)[:, None] >= jnp.arange(GROUP)[None, :]

    def forward(items):
        query_b, key_b, value_b, state_b = items
        probs_lin = rounded(jnp.where(lower, jnp.einsum('ihd,jhd->hij', query_b, key_b), 0.0))
        inner = jnp.einsum('hij,jhd->ihd', probs_lin, value_b)
        return inner + jnp.einsum('ihd,hde->ihe', query_b, state_b, precision=highest)
    lin_out = lax.map(forward, (queries, keys_lin, values_lin, prior)).reshape(TOKENS, WIDTH)
    scaled = grad_normed.astype(jnp.float32) * norm_gain.astype(jnp.float32)[None, :]
    sum_squares = lax.optimization_barrier(jnp.sum(lin_out * lin_out, axis=1, keepdims=True))
    cross = lax.optimization_barrier(jnp.sum(scaled * lin_out, axis=1, keepdims=True))
    root_mean = jnp.sqrt(sum_squares / WIDTH + norm_eps)
    grad_out = rounded(scaled / root_mean - lin_out * cross / (WIDTH * root_mean ** 3)).reshape(shaped)
    later_local = jnp.einsum('ntha,nthb->nhab', queries, grad_out)
    backward_run = jnp.cumsum(later_local[::-1], 0)[::-1]
    after = jnp.concatenate([backward_run[1:], jnp.zeros_like(later_local[:1])], 0)

    def backward(items):
        query_b, key_b, value_b, grad_b, state_b, after_b = items
        probs_lin = rounded(jnp.where(lower, jnp.einsum('ihd,jhd->hij', query_b, key_b), 0.0))
        mix_lin = rounded(jnp.where(lower, jnp.einsum('ihe,jhe->hij', grad_b, value_b), 0.0))
        grad_query = jnp.einsum('hij,jhd->ihd', mix_lin, key_b) + jnp.einsum('ihe,hde->ihd', grad_b, state_b, precision=highest)
        grad_key = jnp.einsum('hij,ihd->jhd', mix_lin, query_b) + jnp.einsum('jhb,hab->jha', value_b, after_b, precision=highest)
        grad_value = jnp.einsum('hij,ihe->jhe', probs_lin, grad_b) + jnp.einsum('jha,hab->jhb', key_b, after_b, precision=highest)
        return (grad_query.astype(jnp.bfloat16), grad_key.astype(jnp.bfloat16), grad_value.astype(jnp.bfloat16))
    grad_query_lin, grad_key_lin, grad_value_lin = lax.map(backward, (queries, keys_lin, values_lin, grad_out, prior, after))
    scale_win = 1.0 / math.sqrt(DH)
    whole = (TOKENS, HEADS, DH)
    query_all = query_win.astype(jnp.float32).reshape(whole)
    grad_all = grad_win.astype(jnp.float32).reshape(whole)
    padding = jnp.zeros((WINDOW, HEADS, DH), jnp.float32)
    key_pad = jnp.concatenate([padding, key_win.astype(jnp.float32).reshape(whole)], 0)
    value_pad = jnp.concatenate([padding, value_win.astype(jnp.float32).reshape(whole)], 0)
    query_pos = jnp.arange(GROUP)[:, None]
    key_pos = jnp.arange(GROUP + WINDOW)[None, :]

    def window_block(index):
        start = (index * GROUP).astype(jnp.int32)
        query_b = lax.dynamic_slice_in_dim(query_all, start, GROUP, 0)
        grad_b = lax.dynamic_slice_in_dim(grad_all, start, GROUP, 0)
        key_b = lax.dynamic_slice_in_dim(key_pad, start, GROUP + WINDOW, 0)
        value_b = lax.dynamic_slice_in_dim(value_pad, start, GROUP + WINDOW, 0)
        allowed = (key_pos > query_pos) & (key_pos <= query_pos + WINDOW) & (key_pos + start >= WINDOW)
        logits = scale_win * jnp.einsum('ihd,jhd->hij', query_b, key_b)
        logits = jnp.where(allowed[None], logits, -1e+30)
        peak = lax.optimization_barrier(jnp.max(logits, axis=2, keepdims=True))
        weights = jnp.exp(logits - peak)
        probs = weights / lax.optimization_barrier(jnp.sum(weights, axis=2, keepdims=True))
        probs_win = rounded(probs)
        win_out = jnp.einsum('hij,jhd->ihd', probs_win, value_b)
        delta = lax.optimization_barrier(jnp.sum(grad_b * win_out, axis=2))
        grad_probs = jnp.einsum('ihd,jhd->hij', grad_b, value_b)
        grad_logits = rounded(probs * (grad_probs - jnp.transpose(delta)[:, :, None]))
        grad_query = scale_win * jnp.einsum('hij,jhd->ihd', grad_logits, key_b)
        grad_key = scale_win * jnp.einsum('hij,ihd->jhd', grad_logits, query_b)
        grad_value = jnp.einsum('hij,ihd->jhd', probs_win, grad_b)
        return (grad_query.astype(jnp.bfloat16), grad_key, grad_value)
    grad_query_win, key_ext, value_ext = lax.map(window_block, jnp.arange(blocks, dtype=jnp.int32))
    return (grad_query_lin.reshape(TOKENS, WIDTH), grad_key_lin.reshape(TOKENS, WIDTH), grad_value_lin.reshape(TOKENS, WIDTH), grad_query_win.reshape(TOKENS, WIDTH), settle(key_ext), settle(value_ext))
```

```python
import functools
import math

import jax
import jax.numpy as jnp
from jax import lax
from jax.experimental import pallas as pl
from jax.experimental.pallas import tpu as pltpu
from jax.sharding import PartitionSpec as P

DH = 128
WINDOW = 512
TILE = 128
ROW = 8
NORM_EPS = 1e-06
HIDDEN = -1e30

f32 = jnp.float32
bf16 = jnp.bfloat16


def dot(left, right, dims):
    return lax.dot_general(left, right, (dims, ((), ())), preferred_element_type=f32)


def dot_nn(left, right):
    return dot(left, right, ((1,), (0,)))


def dot_nt(left, right):
    return dot(left, right, ((1,), (1,)))


def dot_tn(left, right):
    return dot(left, right, ((0,), (0,)))


def halves(value):
    high = value.astype(bf16)
    return high, (value - high.astype(f32)).astype(bf16)


def kernel_call(body, outs, flops, moved, exps=0, scratch=(), limit=12, specs=None):
    return pl.pallas_call(
        body,
        out_shape=outs,
        scratch_shapes=list(scratch),
        compiler_params=pltpu.CompilerParams(vmem_limit_bytes=limit << 20),
        cost_estimate=pl.CostEstimate(
            flops=int(flops), bytes_accessed=int(moved), transcendentals=int(exps)
        ),
        **({"in_specs": specs} if specs else {}),
    )


def shaped(shape, dtype):
    return jax.ShapeDtypeStruct(shape, dtype)


def diagonal_tiles():
    rows = lax.broadcasted_iota(jnp.int32, (TILE, TILE), 0)
    cols = lax.broadcasted_iota(jnp.int32, (TILE, TILE), 1)
    return rows <= cols, rows >= cols


def state_body(key_ref, value_ref, out_ref):
    state = dot_tn(key_ref[...], value_ref[...]).astype(bf16)
    for place in range(out_ref.shape[0]):
        out_ref[place] = state


def total_body(parts_ref, out_ref):
    total = parts_ref[0].astype(f32)
    for place in range(1, parts_ref.shape[0]):
        total = total + parts_ref[place].astype(f32)
    total = total.astype(bf16)
    for place in range(out_ref.shape[0]):
        out_ref[place] = total


def chosen_sum(where_ref, rows_ref, parts_ref, later):
    row, col = where_ref[0], where_ref[1]
    total = None
    for ref, mine in ((rows_ref, row), (parts_ref, col)):
        for place in range(ref.shape[0]):
            wanted = place > mine if later else place < mine
            term = jnp.where(wanted, ref[place].astype(f32), 0.0)
            total = term if total is None else total + term
    return total


def inner_body(query_ref, key_ref, value_ref, out_ref):
    tokens = query_ref.shape[0]
    _, lower = diagonal_tiles()
    for start in range(0, tokens, TILE):
        stop = start + TILE
        query = query_ref[start:stop]
        scores = dot_nt(query, key_ref[start:stop])
        probs = jnp.where(lower, scores, 0.0).astype(bf16)
        result = dot_nn(probs, value_ref[start:stop])
        if start:
            probs = dot_nt(query, key_ref[:start]).astype(bf16)
            result = result + dot_nn(probs, value_ref[:start])
        out_ref[start:stop] = result


def normed_body(
    where_ref, rows_ref, parts_ref, inner_ref, query_ref, grad_ref, gain_ref,
    lin_ref, prior_ref, sums_ref,
):
    prior = chosen_sum(where_ref, rows_ref, parts_ref, False)
    prior_ref[...] = prior
    high, low = halves(prior)
    query = query_ref[...]
    lin_out = inner_ref[...] + dot_nn(query, high) + dot_nn(query, low)
    lin_ref[...] = lin_out
    scaled = grad_ref[...].astype(f32) * gain_ref[...]
    squares, crosses = lin_out * lin_out, scaled * lin_out
    pieces = []
    for terms in (squares, crosses):
        for start in range(0, terms.shape[0], TILE):
            turned = jnp.transpose(terms[start : start + TILE])
            pieces.append(jnp.sum(turned, axis=0, keepdims=True))
    packed = jnp.concatenate(pieces, 0)
    for place in range(sums_ref.shape[0]):
        sums_ref[place] = packed


def grad_out_body(sums_ref, lin_ref, grad_ref, gain_ref, query_ref, out_ref, state_ref, *, width):
    total = sums_ref[0]
    for place in range(1, sums_ref.shape[0]):
        total = total + sums_ref[place]
    groups = total.shape[0] // 2
    inverse = 1.0 / jnp.sqrt(total[:groups] / width + NORM_EPS)
    weight = total[groups:] * inverse * inverse * inverse / width
    turned = jnp.transpose(jnp.concatenate([inverse, weight], 0))
    for group in range(groups):
        tokens = slice(group * TILE, (group + 1) * TILE)
        scaled = grad_ref[tokens].astype(f32) * gain_ref[...]
        grad_out = (
            scaled * turned[:, group : group + 1]
            - lin_ref[tokens] * turned[:, groups + group : groups + group + 1]
        )
        out_ref[tokens] = grad_out.astype(bf16)
    state = dot_tn(query_ref[...], out_ref[...]).astype(bf16)
    for place in range(state_ref.shape[0]):
        state_ref[place] = state


def mixed_body(
    grad_ref, query_ref, key_ref, value_ref, prior_ref, gq_ref, gk_ref, gv_ref,
):
    tokens = query_ref.shape[0]
    upper, lower = diagonal_tiles()
    high, low = halves(prior_ref[...])
    for start in range(0, tokens, TILE):
        stop = start + TILE
        here = slice(start, stop)
        grad, query, key, value = grad_ref[here], query_ref[here], key_ref[here], value_ref[here]
        mix = jnp.where(lower, dot_nt(grad, value), 0.0).astype(bf16)
        result = dot_nn(mix, key) + dot_nt(grad, high) + dot_nt(grad, low)
        if start:
            mix = dot_nt(grad, value_ref[:start]).astype(bf16)
            result = result + dot_nn(mix, key_ref[:start])
        gq_ref[here] = result.astype(bf16)
        mix = jnp.where(upper, dot_nt(value, grad), 0.0).astype(bf16)
        probs = jnp.where(upper, dot_nt(key, query), 0.0).astype(bf16)
        key_part, value_part = dot_nn(mix, query), dot_nn(probs, grad)
        if stop < tokens:
            mix = dot_nt(value, grad_ref[stop:]).astype(bf16)
            probs = dot_nt(key, query_ref[stop:]).astype(bf16)
            key_part = key_part + dot_nn(mix, query_ref[stop:])
            value_part = value_part + dot_nn(probs, grad_ref[stop:])
        gk_ref[here] = key_part
        gv_ref[here] = value_part


def closing_body(
    where_ref, rows_ref, parts_ref, gk_part_ref, gv_part_ref, key_ref, value_ref, gk_ref, gv_ref,
):
    high, low = halves(chosen_sum(where_ref, rows_ref, parts_ref, True))
    key, value = key_ref[...], value_ref[...]
    gk_ref[...] = (gk_part_ref[...] + dot_nt(value, high) + dot_nt(value, low)).astype(bf16)
    gv_ref[...] = (gv_part_ref[...] + dot_nn(key, high) + dot_nn(key, low)).astype(bf16)


def window_body(
    where_ref, query_ref, key_ref, value_ref, grad_ref, halo_ref,
    gq_ref, back_ref, gk_ref, gv_ref, gk_halo, gv_halo,
):
    span = query_ref.shape[0]
    scale = 1.0 / math.sqrt(DH)
    first = where_ref[2] == 0
    upper, _ = diagonal_tiles()
    for start in range(0, span, TILE):
        stop = start + TILE
        here = slice(start, stop)
        query, grad = query_ref[here], grad_ref[here]
        halo_key, halo_value = halo_ref[start:span], halo_ref[span + start :]
        own_key, own_value = key_ref[:stop], value_ref[:stop]
        behind = dot_nt(halo_key, query)
        edge = jnp.where(upper, HIDDEN, behind[:TILE])
        if stop < span:
            behind = jnp.concatenate([edge, behind[TILE:]], 0)
        else:
            behind = edge
        behind = jnp.where(first, HIDDEN, behind)
        own = dot_nt(own_key, query)
        edge = jnp.where(upper, own[start:], HIDDEN)
        own = jnp.concatenate([own[:start], edge], 0) if start else edge
        peak = jnp.maximum(
            jnp.max(behind, axis=0, keepdims=True), jnp.max(own, axis=0, keepdims=True)
        )
        behind = jnp.exp((behind - peak) * scale)
        own = jnp.exp((own - peak) * scale)
        total = jnp.sum(behind, axis=0, keepdims=True) + jnp.sum(own, axis=0, keepdims=True)
        inverse = 1.0 / total
        behind, own = behind * inverse, own * inverse
        behind_win, own_win = behind.astype(bf16), own.astype(bf16)
        behind_grad = dot_nt(halo_value, grad)
        own_grad = dot_nt(own_value, grad)
        delta = jnp.sum(behind_win.astype(f32) * behind_grad, axis=0, keepdims=True) + jnp.sum(
            own_win.astype(f32) * own_grad, axis=0, keepdims=True
        )
        behind_logit = (behind * (behind_grad - delta)).astype(bf16)
        own_logit = (own * (own_grad - delta)).astype(bf16)
        result = dot_tn(halo_key, behind_logit) + dot_tn(own_key, own_logit)
        gq_ref[here] = (jnp.transpose(result) * scale).astype(bf16)
        for out, rows, terms in (
            (gk_halo, slice(start, span), dot_nn(behind_logit, query) * scale),
            (gv_halo, slice(start, span), dot_nn(behind_win, grad)),
            (gk_ref, slice(0, stop), dot_nn(own_logit, query) * scale),
            (gv_ref, slice(0, stop), dot_nn(own_win, grad)),
        ):
            if out is gk_halo or out is gv_halo:
                if start:
                    out[rows] += terms
                else:
                    out[rows] = terms
            else:
                if start:
                    out[:start] += terms[:start]
                out[here] = terms[start:]
    back_ref[:span] = gk_halo[...].astype(bf16)
    back_ref[span:] = gv_halo[...].astype(bf16)


def settle_body(gk_ref, gv_ref, back_ref, gk_out, gv_out):
    span = gk_ref.shape[0]
    gk_out[...] = (gk_ref[...] + back_ref[:span].astype(f32)).astype(bf16)
    gv_out[...] = (gv_ref[...] + back_ref[span:].astype(f32)).astype(bf16)


def local(
    query_lin, key_lin, value_lin, norm_gain, grad_normed, query_win, key_win, value_win, grad_win
):
    tokens, width = query_lin.shape
    blocks, heads = lax.axis_size("ctx"), lax.axis_size("head")
    rows = blocks // ROW
    my_index = lax.axis_index("ctx")
    where = jnp.stack([my_index // ROW, my_index % ROW, my_index]).astype(jnp.int32)
    row_groups = [[row * ROW + col for col in range(ROW)] for row in range(rows)]
    col_groups = [[row * ROW + col for row in range(rows)] for col in range(ROW)]
    gain = norm_gain.reshape(1, width)
    state = (DH, DH)
    block = (tokens, width)
    macs = tokens * DH * DH
    square = tokens * tokens * DH
    size = tokens * DH * 2
    in_smem = pl.BlockSpec(memory_space=pltpu.SMEM)
    in_vmem = pl.BlockSpec(memory_space=pltpu.VMEM)

    def along_row(value):
        return lax.all_to_all(value, "ctx", 0, 0, axis_index_groups=row_groups)

    def along_col(value):
        return lax.all_to_all(value, "ctx", 0, 0, axis_index_groups=col_groups)

    def row_total(parts):
        return kernel_call(
            total_body, shaped((rows,) + state, bf16), 8 * DH * DH, 16 * DH * DH * 2
        )(parts)

    def shift(value, steps):
        first, last = max(0, -steps), min(blocks, blocks - steps)
        return lax.ppermute(value, "ctx", [(at, at + steps) for at in range(first, last)])

    own_state = kernel_call(
        state_body, shaped((ROW,) + state, bf16), 2 * macs, 2 * size + ROW * DH * DH * 2
    )(key_lin, value_lin)
    parts = along_row(own_state)
    halo = shift(jnp.concatenate([key_win, value_win], 0), 1)
    inner = kernel_call(inner_body, shaped(block, f32), 2.5 * square, 5 * size)(
        query_lin, key_lin, value_lin
    )
    row_parts = along_col(row_total(parts))
    gq_win, back, gk_own, gv_own = kernel_call(
        window_body,
        (shaped(block, bf16), shaped((2 * tokens, width), bf16), shaped(block, f32), shaped(block, f32)),
        12.5 * square,
        13 * size,
        tokens * tokens,
        (pltpu.VMEM(block, f32), pltpu.VMEM(block, f32)),
        16,
        [in_smem] + [in_vmem] * 5,
    )(where, query_win, key_win, value_win, grad_win, halo)
    lin_out, prior, sums = kernel_call(
        normed_body,
        (shaped(block, f32), shaped(state, f32), shaped((heads, 8, TILE), f32)),
        4 * macs,
        8 * size,
        specs=[in_smem] + [in_vmem] * 6,
    )(where, row_parts, parts, inner, query_lin, grad_normed, gain)
    all_sums = lax.all_to_all(sums, "head", 0, 0)
    returned = shift(back, -1)
    grad_out, later_state = kernel_call(
        functools.partial(grad_out_body, width=float(width * heads)),
        (shaped(block, bf16), shaped((ROW,) + state, bf16)),
        2 * macs,
        8 * size,
    )(all_sums, lin_out, grad_normed, gain, query_lin)
    later_parts = along_row(later_state)
    gq_lin, gk_part, gv_part = kernel_call(
        mixed_body, (shaped(block, bf16), shaped(block, f32), shaped(block, f32)), 7 * square, 10 * size
    )(grad_out, query_lin, key_lin, value_lin, prior)
    later_rows = along_col(row_total(later_parts))
    gk_win, gv_win = kernel_call(settle_body, (shaped(block, bf16),) * 2, tokens * DH, 8 * size)(
        gk_own, gv_own, returned
    )
    gk_lin, gv_lin = kernel_call(
        closing_body,
        (shaped(block, bf16),) * 2,
        8 * macs,
        8 * size,
        specs=[in_smem] + [in_vmem] * 6,
    )(where, later_rows, later_parts, gk_part, gv_part, key_lin, value_lin)
    return gq_lin, gk_lin, gv_lin, gq_win, gk_win, gv_win


def solution(mesh):
    placed = P("ctx", "head")
    return jax.shard_map(
        local,
        mesh=mesh,
        in_specs=(placed, placed, placed, P("head")) + (placed,) * 5,
        out_specs=(placed,) * 6,
        check_vma=False,
    )
```

```python
import functools
import math

import jax
import jax.numpy as jnp
from jax import lax
from jax.experimental import pallas as pl
from jax.experimental.pallas import tpu as pltpu
from jax.sharding import PartitionSpec as P

DH = 128
WINDOW = 512
TILE = 128
ROW = 8
NORM_EPS = 1e-06
HIDDEN = -1e30
LONG = 4e9

f32 = jnp.float32
bf16 = jnp.bfloat16


def dot(left, right, dims):
    return lax.dot_general(left, right, (dims, ((), ())), preferred_element_type=f32)


def dot_nn(left, right):
    return dot(left, right, ((1,), (0,)))


def dot_nt(left, right):
    return dot(left, right, ((1,), (1,)))


def dot_tn(left, right):
    return dot(left, right, ((0,), (0,)))


def halves(value):
    high = value.astype(bf16)
    return high, (value - high.astype(f32)).astype(bf16)


def kernel_call(
    body, outs, flops, moved, exps=0, scratch=(), limit=12, specs=None, out_specs=None, ahead=0
):
    def run(*refs):
        inputs = len(specs)
        body(*refs[: inputs - ahead], *refs[inputs:])

    return pl.pallas_call(
        run if ahead else body,
        name=getattr(body, "func", body).__name__,
        out_shape=outs,
        scratch_shapes=list(scratch),
        compiler_params=pltpu.CompilerParams(vmem_limit_bytes=limit << 20),
        cost_estimate=pl.CostEstimate(
            flops=int(flops), bytes_accessed=int(moved), transcendentals=int(exps)
        ),
        **({"in_specs": specs} if specs else {}),
        **({"out_specs": out_specs} if out_specs else {}),
    )


def shaped(shape, dtype):
    return jax.ShapeDtypeStruct(shape, dtype)


def diagonal_tiles():
    rows = lax.broadcasted_iota(jnp.int32, (TILE, TILE), 0)
    cols = lax.broadcasted_iota(jnp.int32, (TILE, TILE), 1)
    return rows <= cols, rows >= cols


def state_body(key_hbm, value_hbm, out_ref, done_ref, key_ref, value_ref, arrived):
    copies = []
    for start in range(0, key_ref.shape[0], TILE):
        here = pl.ds(start, TILE)
        for far, local_ref in ((key_hbm, key_ref), (value_hbm, value_ref)):
            copy = pltpu.make_async_copy(far.at[here], local_ref.at[here], arrived.at[len(copies)])
            copy.start()
            copies.append(copy)
    for copy in copies:
        copy.wait()
    state = dot_tn(key_ref[...], value_ref[...]).astype(bf16)
    for place in range(out_ref.shape[0]):
        out_ref[place] = state
    done_ref[...] = jnp.zeros_like(done_ref)


def spread(value, near, far, sent):
    near[...] = value
    copies = [
        pltpu.make_async_copy(near, far.at[place], sent.at[place]) for place in range(far.shape[0])
    ]
    for copy in copies:
        copy.start()
    return copies


def total_body(parts_ref, out_hbm, near, sent):
    total = parts_ref[0].astype(f32)
    for place in range(1, parts_ref.shape[0]):
        total = total + parts_ref[place].astype(f32)
    for copy in spread(total.astype(bf16), near, out_hbm, sent):
        copy.wait()


def pack_body(key_ref, value_ref, out_ref):
    span = key_ref.shape[0]
    out_ref[:span] = key_ref[...]
    out_ref[span:] = value_ref[...]


def chosen_sum(where_ref, rows_ref, parts_ref, later):
    row, col = where_ref[0], where_ref[1]
    total = None
    for ref, mine in ((rows_ref, row), (parts_ref, col)):
        for place in range(ref.shape[0]):
            wanted = place > mine if later else place < mine
            term = jnp.where(wanted, ref[place].astype(f32), 0.0)
            total = term if total is None else total + term
    return total


def inner_body(query_ref, key_ref, value_ref, grad_ref, gain_ref, out_ref, scaled_ref):
    tokens = query_ref.shape[0]
    _, lower = diagonal_tiles()
    for start in range(0, tokens, TILE):
        stop = start + TILE
        query = query_ref[start:stop]
        scores = dot_nt(query, key_ref[start:stop])
        probs = jnp.where(lower, scores, 0.0).astype(bf16)
        result = dot_nn(probs, value_ref[start:stop])
        if start:
            probs = dot_nt(query, key_ref[:start]).astype(bf16)
            result = result + dot_nn(probs, value_ref[:start])
        out_ref[start:stop] = result
    scaled_ref[...] = grad_ref[...].astype(f32) * gain_ref[...]


def normed_body(
    where_ref, rows_ref, parts_ref, inner_ref, query_ref, scaled_ref,
    lin_ref, prior_ref, sums_hbm, near, sent,
):
    prior = chosen_sum(where_ref, rows_ref, parts_ref, False)
    prior_ref[...] = prior
    high, low = halves(prior)
    squares, crosses = [], []
    for start in range(0, query_ref.shape[0], TILE):
        here = slice(start, start + TILE)
        query = query_ref[here]
        lin_out = inner_ref[here] + dot_nn(query, high) + dot_nn(query, low)
        lin_ref[here] = lin_out
        for terms, pieces in ((lin_out, squares), (scaled_ref[here], crosses)):
            turned = jnp.transpose(terms * lin_out)
            pieces.append(jnp.sum(turned, axis=0, keepdims=True))
    for copy in spread(jnp.concatenate(squares + crosses, 0), near, sums_hbm, sent):
        copy.wait()


def grad_out_body(
    sums_ref, lin_ref, scaled_ref, query_ref, out_ref, state_ref, *, width
):
    total = sums_ref[0]
    for place in range(1, sums_ref.shape[0]):
        total = total + sums_ref[place]
    groups = total.shape[0] // 2
    inverse = 1.0 / jnp.sqrt(total[:groups] / width + NORM_EPS)
    weight = total[groups:] * inverse * inverse * inverse / width
    turned = jnp.transpose(jnp.concatenate([inverse, weight], 0))
    for group in range(groups):
        tokens = slice(group * TILE, (group + 1) * TILE)
        grad_out = (
            scaled_ref[tokens] * turned[:, group : group + 1]
            - lin_ref[tokens] * turned[:, groups + group : groups + group + 1]
        )
        out_ref[tokens] = grad_out.astype(bf16)
    state = dot_tn(query_ref[...], out_ref[...]).astype(bf16)
    for place in range(state_ref.shape[0]):
        state_ref[place] = state


def probs_body(query_ref, key_ref, value_ref, out_ref, kept_ref):
    tokens = query_ref.shape[0]
    upper, _ = diagonal_tiles()
    for start in range(0, tokens, TILE):
        stop = start + TILE
        here = slice(start, stop)
        key = key_ref[here]
        out_ref[here, here] = jnp.where(upper, dot_nt(key, query_ref[here]), 0.0).astype(bf16)
        if stop < tokens:
            out_ref[here, stop:] = dot_nt(key, query_ref[stop:]).astype(bf16)
    kept_ref[:tokens] = key_ref[...]
    kept_ref[tokens:] = value_ref[...]


def mixed_body(
    grad_ref, query_ref, kept_ref, probs_ref, prior_ref, gq_ref, gk_ref, gv_ref,
):
    tokens = query_ref.shape[0]
    upper, lower = diagonal_tiles()
    high, low = halves(prior_ref[...])
    for start in range(0, tokens, TILE):
        stop = start + TILE
        here = slice(start, stop)
        grad, query = grad_ref[here], query_ref[here]
        key, value = kept_ref[here], kept_ref[tokens + start : tokens + stop]
        mix = jnp.where(lower, dot_nt(grad, value), 0.0).astype(bf16)
        result = dot_nn(mix, key) + dot_nt(grad, high) + dot_nt(grad, low)
        if start:
            mix = dot_nt(grad, kept_ref[tokens : tokens + start]).astype(bf16)
            result = result + dot_nn(mix, kept_ref[:start])
        gq_ref[here] = result.astype(bf16)
        mix = jnp.where(upper, dot_nt(value, grad), 0.0).astype(bf16)
        key_part = dot_nn(mix, query)
        if stop < tokens:
            mix = dot_nt(value, grad_ref[stop:]).astype(bf16)
            key_part = key_part + dot_nn(mix, query_ref[stop:])
        gk_ref[here] = key_part
        gv_ref[here] = dot_nn(probs_ref[here, start:], grad_ref[start:])


def closing_body(
    where_ref, rows_ref, parts_ref, gk_part_ref, gv_part_ref, kept_ref,
    gk_hbm, gv_hbm, gk_ref, gv_ref, sent,
):
    high, low = halves(chosen_sum(where_ref, rows_ref, parts_ref, True))
    copies = []
    tokens = gk_ref.shape[0]
    for start in range(0, tokens, 2 * TILE):
        here = pl.ds(start, 2 * TILE)
        key, value = kept_ref[here], kept_ref[pl.ds(tokens + start, 2 * TILE)]
        gk_ref[here] = (gk_part_ref[here] + dot_nt(value, high) + dot_nt(value, low)).astype(bf16)
        gv_ref[here] = (gv_part_ref[here] + dot_nn(key, high) + dot_nn(key, low)).astype(bf16)
        for near, far in ((gk_ref, gk_hbm), (gv_ref, gv_hbm)):
            copy = pltpu.make_async_copy(near.at[here], far.at[here], sent.at[len(copies)])
            copy.start()
            copies.append(copy)
    for copy in copies:
        copy.wait()


def window_body(
    where_ref, query_ref, key_ref, value_ref, grad_ref, halo_ref,
    back_ref, behind_logit_ref, own_logit_ref, own_win_ref, behind_win_ref,
):
    span = query_ref.shape[0]
    scale = 1.0 / math.sqrt(DH)
    first = where_ref[2] == 0
    upper, _ = diagonal_tiles()
    for start in range(0, span, TILE):
        stop = start + TILE
        here = slice(start, stop)
        query, grad = query_ref[here], grad_ref[here]
        behind = dot_nt(halo_ref[start:span], query)
        edge = jnp.where(upper, HIDDEN, behind[:TILE])
        behind = jnp.concatenate([edge, behind[TILE:]], 0) if stop < span else edge
        behind = jnp.where(first, HIDDEN, behind)
        own = dot_nt(key_ref[:stop], query)
        edge = jnp.where(upper, own[start:], HIDDEN)
        own = jnp.concatenate([own[:start], edge], 0) if start else edge
        peak = jnp.maximum(
            jnp.max(behind, axis=0, keepdims=True), jnp.max(own, axis=0, keepdims=True)
        )
        behind = jnp.exp((behind - peak) * scale)
        own = jnp.exp((own - peak) * scale)
        total = jnp.sum(behind, axis=0, keepdims=True) + jnp.sum(own, axis=0, keepdims=True)
        inverse = 1.0 / total
        behind, own = behind * inverse, own * inverse
        behind_win, own_win = behind.astype(bf16), own.astype(bf16)
        behind_grad = dot_nt(halo_ref[span + start :], grad)
        own_grad = dot_nt(value_ref[:stop], grad)
        delta = jnp.sum(behind_win.astype(f32) * behind_grad, axis=0, keepdims=True) + jnp.sum(
            own_win.astype(f32) * own_grad, axis=0, keepdims=True
        )
        behind_win_ref[start:, here] = behind_win
        own_win_ref[:stop, here] = own_win
        behind_logit_ref[start:, here] = (behind * (behind_grad - delta)).astype(bf16)
        own_logit_ref[:stop, here] = (own * (own_grad - delta)).astype(bf16)
    for start in range(0, span, TILE):
        stop = start + TILE
        here = slice(start, stop)
        back = dot_nn(behind_logit_ref[here, :stop], query_ref[:stop]) * scale
        back_ref[here] = back.astype(bf16)
        back = dot_nn(behind_win_ref[here, :stop], grad_ref[:stop])
        back_ref[span + start : span + stop] = back.astype(bf16)


def own_body(
    behind_logit_ref, own_logit_ref, own_win_ref, halo_ref, query_ref, key_ref, grad_ref,
    gq_ref, gk_ref, gv_ref,
):
    span = query_ref.shape[0]
    scale = 1.0 / math.sqrt(DH)
    for start in range(0, span, TILE):
        stop = start + TILE
        here = slice(start, stop)
        result = dot_tn(halo_ref[start:span], behind_logit_ref[start:, here])
        result = result + dot_tn(key_ref[:stop], own_logit_ref[:stop, here])
        gq_ref[here] = (jnp.transpose(result) * scale).astype(bf16)
        gk_ref[here] = dot_nn(own_logit_ref[here, start:], query_ref[start:]) * scale
        gv_ref[here] = dot_nn(own_win_ref[here, start:], grad_ref[start:])


def settle_body(gk_ref, gv_ref, back_ref, gk_out, gv_out, done_ref):
    span = gk_ref.shape[0]
    gk_out[...] = (gk_ref[...] + back_ref[:span].astype(f32)).astype(bf16)
    gv_out[...] = (gv_ref[...] + back_ref[span:].astype(f32)).astype(bf16)
    done_ref[...] = jnp.zeros_like(done_ref)


def local(
    query_lin, key_lin, value_lin, norm_gain, grad_normed, query_win, key_win, value_win, grad_win
):
    tokens, width = query_lin.shape
    blocks, heads = lax.axis_size("ctx"), lax.axis_size("head")
    rows = blocks // ROW
    my_index = lax.axis_index("ctx")
    where = jnp.stack([my_index // ROW, my_index % ROW, my_index]).astype(jnp.int32)
    row_groups = [[row * ROW + col for col in range(ROW)] for row in range(rows)]
    col_groups = [[row * ROW + col for row in range(rows)] for col in range(ROW)]
    gain = norm_gain.reshape(1, width)
    state = (DH, DH)
    block = (tokens, width)
    macs = tokens * DH * DH
    square = tokens * tokens * DH
    size = tokens * DH * 2
    in_smem = pl.BlockSpec(memory_space=pltpu.SMEM)
    in_vmem = pl.BlockSpec(memory_space=pltpu.VMEM)
    in_hbm = pl.BlockSpec(memory_space=pltpu.HBM)
    anywhere = pl.BlockSpec(memory_space=pl.ANY)
    copies = pltpu.SemaphoreType.DMA((ROW,))
    spreading = (pltpu.VMEM(state, bf16), pltpu.SemaphoreType.DMA((max(rows, ROW),)))

    def along_row(value):
        return lax.all_to_all(value, "ctx", 0, 0, axis_index_groups=row_groups)

    def along_col(value):
        return lax.all_to_all(value, "ctx", 0, 0, axis_index_groups=col_groups)

    def row_total(parts, flops, *ahead):
        return kernel_call(
            total_body,
            shaped((rows,) + state, bf16),
            flops,
            16 * DH * DH * 2,
            scratch=spreading,
            specs=[in_vmem] + [anywhere] * len(ahead),
            out_specs=in_hbm,
            ahead=len(ahead),
        )(parts, *ahead)

    def shift(value, steps):
        first, last = max(0, -steps), min(blocks, blocks - steps)
        return lax.ppermute(value, "ctx", [(at, at + steps) for at in range(first, last)])

    own_state, started = kernel_call(
        state_body,
        (shaped((ROW,) + state, bf16), shaped((8, TILE), f32)),
        2 * macs,
        2 * size + ROW * DH * DH * 2,
        scratch=(pltpu.VMEM(block, bf16), pltpu.VMEM(block, bf16), copies),
        limit=60,
        specs=[in_hbm] * 2,
    )(key_lin, value_lin)
    parts = along_row(own_state)
    row_sum = row_total(parts, LONG / 4)
    halo_pack = kernel_call(
        pack_body,
        shaped((2 * tokens, width), bf16),
        0,
        4 * size,
        specs=[in_vmem] * 2 + [anywhere],
        ahead=1,
    )(key_win, value_win, started)
    halo = shift(halo_pack, 1)
    inner, scaled = kernel_call(
        inner_body,
        (shaped(block, f32), shaped(block, f32)),
        LONG,
        8 * size,
        specs=[in_vmem] * 5 + [anywhere] * 2,
        ahead=2,
    )(query_lin, key_lin, value_lin, grad_normed, gain, row_sum, halo)
    row_parts = along_col(row_sum)
    lin_out, prior, sums = kernel_call(
        normed_body,
        (shaped(block, f32), shaped(state, f32), shaped((heads, 8, TILE), f32)),
        4 * macs,
        8 * size,
        scratch=(pltpu.VMEM((8, TILE), f32), pltpu.SemaphoreType.DMA((heads,))),
        specs=[in_smem] + [in_vmem] * 5 + [anywhere],
        out_specs=(in_vmem, in_vmem, in_hbm),
        ahead=1,
    )(where, row_parts, parts, inner, query_lin, scaled, halo)
    flat = shaped((tokens, tokens), bf16)
    back, behind_logit, own_logit, own_win = kernel_call(
        window_body,
        (shaped((2 * tokens, width), bf16), flat, flat, flat),
        8 * square,
        20 * size,
        tokens * tokens,
        (pltpu.VMEM((tokens, tokens), bf16),),
        16,
        [in_smem] + [in_vmem] * 5 + [anywhere],
        ahead=1,
    )(where, query_win, key_win, value_win, grad_win, halo, sums)
    gq_win, gk_own, gv_own = kernel_call(
        own_body,
        (shaped(block, bf16), shaped(block, f32), shaped(block, f32)),
        5 * square,
        20 * size,
        specs=[in_vmem] * 7,
    )(behind_logit, own_logit, own_win, halo, query_win, key_win, grad_win)
    all_sums = lax.all_to_all(sums, "head", 0, 0)
    returned = shift(back, -1)
    probs, kept = kernel_call(
        probs_body,
        (shaped((tokens, tokens), bf16), shaped((2 * tokens, width), bf16)),
        LONG,
        8 * size,
        specs=[in_vmem] * 3 + [anywhere],
        ahead=1,
    )(query_lin, key_lin, value_lin, sums)
    grad_out, later_state = kernel_call(
        functools.partial(grad_out_body, width=float(width * heads)),
        (shaped(block, bf16), shaped((ROW,) + state, bf16)),
        2 * macs,
        8 * size,
        specs=[in_vmem] * 4 + [anywhere] * 3,
        ahead=3,
    )(all_sums, lin_out, scaled, query_lin, returned, probs, gk_own)
    later_parts = along_row(later_state)
    later_sum = row_total(later_parts, 8 * DH * DH)
    gq_lin, gk_part, gv_part = kernel_call(
        mixed_body,
        (shaped(block, bf16), shaped(block, f32), shaped(block, f32)),
        5 * square,
        10 * size,
        specs=[in_vmem] * 5 + [anywhere],
        ahead=1,
    )(grad_out, query_lin, kept, probs, prior, later_sum)
    later_rows = along_col(later_sum)
    gk_win, gv_win, settled = kernel_call(
        settle_body,
        (shaped(block, bf16), shaped(block, bf16), shaped((8, TILE), f32)),
        tokens * DH,
        8 * size,
        specs=[in_vmem] * 3 + [anywhere],
        ahead=1,
    )(gk_own, gv_own, returned, later_sum)
    gk_lin, gv_lin = kernel_call(
        closing_body,
        (shaped(block, bf16),) * 2,
        8 * macs,
        8 * size,
        scratch=(pltpu.VMEM(block, bf16), pltpu.VMEM(block, bf16), copies),
        specs=[in_smem] + [in_vmem] * 5 + [anywhere],
        out_specs=(in_hbm, in_hbm),
        ahead=1,
    )(where, later_rows, later_parts, gk_part, gv_part, kept, settled)
    return gq_lin, gk_lin, gv_lin, gq_win, gk_win, gv_win


def solution(mesh):
    placed = P("ctx", "head")
    return jax.shard_map(
        local,
        mesh=mesh,
        in_specs=(placed, placed, placed, P("head")) + (placed,) * 5,
        out_specs=(placed,) * 6,
        check_vma=False,
    )
```

```python
import functools
import math

import jax
import jax.numpy as jnp
from jax import lax
from jax.experimental import pallas as pl
from jax.experimental.pallas import tpu as pltpu
from jax.sharding import PartitionSpec as P

DH = 128
WINDOW = 512
TILE = 128
ROW = 8
NORM_EPS = 1e-06
HIDDEN = -1e30
LONG = 4e9

f32 = jnp.float32
bf16 = jnp.bfloat16


def dot(left, right, dims):
    return lax.dot_general(left, right, (dims, ((), ())), preferred_element_type=f32)


def dot_nn(left, right):
    return dot(left, right, ((1,), (0,)))


def dot_nt(left, right):
    return dot(left, right, ((1,), (1,)))


def dot_tn(left, right):
    return dot(left, right, ((0,), (0,)))


def halves(value):
    high = value.astype(bf16)
    return high, (value - high.astype(f32)).astype(bf16)


def kernel_call(
    body, outs, flops, moved, exps=0, scratch=(), limit=12, specs=None, out_specs=None, ahead=0
):
    def run(*refs):
        inputs = len(specs)
        body(*refs[: inputs - ahead], *refs[inputs:])

    return pl.pallas_call(
        run if ahead else body,
        name=getattr(body, "func", body).__name__,
        out_shape=outs,
        scratch_shapes=list(scratch),
        compiler_params=pltpu.CompilerParams(vmem_limit_bytes=limit << 20),
        cost_estimate=pl.CostEstimate(
            flops=int(flops), bytes_accessed=int(moved), transcendentals=int(exps)
        ),
        **({"in_specs": specs} if specs else {}),
        **({"out_specs": out_specs} if out_specs else {}),
    )


def shaped(shape, dtype):
    return jax.ShapeDtypeStruct(shape, dtype)


def diagonal_tiles():
    rows = lax.broadcasted_iota(jnp.int32, (TILE, TILE), 0)
    cols = lax.broadcasted_iota(jnp.int32, (TILE, TILE), 1)
    return rows <= cols, rows >= cols


def warm_body(where_ref, out_ref):
    out_ref[...] = jnp.zeros_like(out_ref) + where_ref[0].astype(f32)


def state_body(key_ref, value_ref, out_ref):
    state = dot_tn(key_ref[...], value_ref[...]).astype(bf16)
    for place in range(out_ref.shape[0]):
        out_ref[place] = state


def spread(value, near, far, sent):
    near[...] = value
    copies = [
        pltpu.make_async_copy(near, far.at[place], sent.at[place]) for place in range(far.shape[0])
    ]
    for copy in copies:
        copy.start()
    return copies


def total_body(parts_ref, out_hbm, near, sent):
    total = parts_ref[0].astype(f32)
    for place in range(1, parts_ref.shape[0]):
        total = total + parts_ref[place].astype(f32)
    for copy in spread(total.astype(bf16), near, out_hbm, sent):
        copy.wait()


def pack_body(key_ref, value_ref, out_ref):
    span = key_ref.shape[0]
    out_ref[:span] = key_ref[...]
    out_ref[span:] = value_ref[...]


def chosen_sum(where_ref, rows_ref, parts_ref, later):
    row, col = where_ref[0], where_ref[1]
    total = None
    for ref, mine in ((rows_ref, row), (parts_ref, col)):
        for place in range(ref.shape[0]):
            wanted = place > mine if later else place < mine
            term = jnp.where(wanted, ref[place].astype(f32), 0.0)
            total = term if total is None else total + term
    return total


def inner_body(query_ref, key_ref, value_ref, grad_ref, gain_ref, out_ref, scaled_ref):
    tokens = query_ref.shape[0]
    _, lower = diagonal_tiles()
    for start in range(0, tokens, TILE):
        stop = start + TILE
        query = query_ref[start:stop]
        scores = dot_nt(query, key_ref[start:stop])
        probs = jnp.where(lower, scores, 0.0).astype(bf16)
        result = dot_nn(probs, value_ref[start:stop])
        if start:
            probs = dot_nt(query, key_ref[:start]).astype(bf16)
            result = result + dot_nn(probs, value_ref[:start])
        out_ref[start:stop] = result
    scaled_ref[...] = grad_ref[...].astype(f32) * gain_ref[...]


def normed_body(
    where_ref, rows_ref, parts_ref, inner_ref, query_ref, scaled_ref,
    lin_ref, prior_ref, sums_hbm, near, sent,
):
    prior = chosen_sum(where_ref, rows_ref, parts_ref, False)
    prior_ref[...] = prior
    high, low = halves(prior)
    squares, crosses = [], []
    for start in range(0, query_ref.shape[0], TILE):
        here = slice(start, start + TILE)
        query = query_ref[here]
        lin_out = inner_ref[here] + dot_nn(query, high) + dot_nn(query, low)
        lin_ref[here] = lin_out
        for terms, pieces in ((lin_out, squares), (scaled_ref[here], crosses)):
            turned = jnp.transpose(terms * lin_out)
            pieces.append(jnp.sum(turned, axis=0, keepdims=True))
    for copy in spread(jnp.concatenate(squares + crosses, 0), near, sums_hbm, sent):
        copy.wait()


def grad_out_body(
    sums_ref, lin_ref, scaled_ref, query_ref, out_ref, state_ref, *, width
):
    total = sums_ref[0]
    for place in range(1, sums_ref.shape[0]):
        total = total + sums_ref[place]
    groups = total.shape[0] // 2
    inverse = 1.0 / jnp.sqrt(total[:groups] / width + NORM_EPS)
    weight = total[groups:] * inverse * inverse * inverse / width
    turned = jnp.transpose(jnp.concatenate([inverse, weight], 0))
    for group in range(groups):
        tokens = slice(group * TILE, (group + 1) * TILE)
        grad_out = (
            scaled_ref[tokens] * turned[:, group : group + 1]
            - lin_ref[tokens] * turned[:, groups + group : groups + group + 1]
        )
        out_ref[tokens] = grad_out.astype(bf16)
    state = dot_tn(query_ref[...], out_ref[...]).astype(bf16)
    for place in range(state_ref.shape[0]):
        state_ref[place] = state


def probs_body(query_ref, key_ref, value_ref, out_ref, kept_ref):
    tokens = query_ref.shape[0]
    upper, _ = diagonal_tiles()
    for start in range(0, tokens, TILE):
        stop = start + TILE
        here = slice(start, stop)
        key = key_ref[here]
        out_ref[here, here] = jnp.where(upper, dot_nt(key, query_ref[here]), 0.0).astype(bf16)
        if stop < tokens:
            out_ref[here, stop:] = dot_nt(key, query_ref[stop:]).astype(bf16)
    kept_ref[:tokens] = key_ref[...]
    kept_ref[tokens:] = value_ref[...]


def mixed_body(
    grad_ref, query_ref, kept_ref, probs_ref, prior_ref, gq_ref, gk_ref, gv_ref,
):
    tokens = query_ref.shape[0]
    upper, lower = diagonal_tiles()
    high, low = halves(prior_ref[...])
    for start in range(0, tokens, TILE):
        stop = start + TILE
        here = slice(start, stop)
        grad, query = grad_ref[here], query_ref[here]
        key, value = kept_ref[here], kept_ref[tokens + start : tokens + stop]
        mix = jnp.where(lower, dot_nt(grad, value), 0.0).astype(bf16)
        result = dot_nn(mix, key) + dot_nt(grad, high) + dot_nt(grad, low)
        if start:
            mix = dot_nt(grad, kept_ref[tokens : tokens + start]).astype(bf16)
            result = result + dot_nn(mix, kept_ref[:start])
        gq_ref[here] = result.astype(bf16)
        mix = jnp.where(upper, dot_nt(value, grad), 0.0).astype(bf16)
        key_part = dot_nn(mix, query)
        if stop < tokens:
            mix = dot_nt(value, grad_ref[stop:]).astype(bf16)
            key_part = key_part + dot_nn(mix, query_ref[stop:])
        gk_ref[here] = key_part
        gv_ref[here] = dot_nn(probs_ref[here, start:], grad_ref[start:])


def closing_body(
    where_ref, rows_ref, parts_ref, gk_part_ref, gv_part_ref, kept_ref,
    gk_hbm, gv_hbm, gk_ref, gv_ref, sent,
):
    high, low = halves(chosen_sum(where_ref, rows_ref, parts_ref, True))
    copies = []
    tokens = gk_ref.shape[0]
    for start in range(0, tokens, 2 * TILE):
        here = pl.ds(start, 2 * TILE)
        key, value = kept_ref[here], kept_ref[pl.ds(tokens + start, 2 * TILE)]
        gk_ref[here] = (gk_part_ref[here] + dot_nt(value, high) + dot_nt(value, low)).astype(bf16)
        gv_ref[here] = (gv_part_ref[here] + dot_nn(key, high) + dot_nn(key, low)).astype(bf16)
        for near, far in ((gk_ref, gk_hbm), (gv_ref, gv_hbm)):
            copy = pltpu.make_async_copy(near.at[here], far.at[here], sent.at[len(copies)])
            copy.start()
            copies.append(copy)
    for copy in copies:
        copy.wait()


def window_body(
    where_ref, query_ref, key_ref, value_ref, grad_ref, halo_ref,
    back_ref, behind_logit_ref, own_logit_ref, own_win_ref, behind_win_ref,
):
    span = query_ref.shape[0]
    scale = 1.0 / math.sqrt(DH)
    first = where_ref[2] == 0
    upper, _ = diagonal_tiles()
    for start in range(0, span, TILE):
        stop = start + TILE
        here = slice(start, stop)
        query, grad = query_ref[here], grad_ref[here]
        behind = dot_nt(halo_ref[start:span], query)
        edge = jnp.where(upper, HIDDEN, behind[:TILE])
        behind = jnp.concatenate([edge, behind[TILE:]], 0) if stop < span else edge
        behind = jnp.where(first, HIDDEN, behind)
        own = dot_nt(key_ref[:stop], query)
        edge = jnp.where(upper, own[start:], HIDDEN)
        own = jnp.concatenate([own[:start], edge], 0) if start else edge
        peak = jnp.maximum(
            jnp.max(behind, axis=0, keepdims=True), jnp.max(own, axis=0, keepdims=True)
        )
        behind = jnp.exp((behind - peak) * scale)
        own = jnp.exp((own - peak) * scale)
        total = jnp.sum(behind, axis=0, keepdims=True) + jnp.sum(own, axis=0, keepdims=True)
        inverse = 1.0 / total
        behind, own = behind * inverse, own * inverse
        behind_win, own_win = behind.astype(bf16), own.astype(bf16)
        behind_grad = dot_nt(halo_ref[span + start :], grad)
        own_grad = dot_nt(value_ref[:stop], grad)
        delta = jnp.sum(behind_win.astype(f32) * behind_grad, axis=0, keepdims=True) + jnp.sum(
            own_win.astype(f32) * own_grad, axis=0, keepdims=True
        )
        behind_win_ref[start:, here] = behind_win
        own_win_ref[:stop, here] = own_win
        behind_logit_ref[start:, here] = (behind * (behind_grad - delta)).astype(bf16)
        own_logit_ref[:stop, here] = (own * (own_grad - delta)).astype(bf16)
    for start in range(0, span, TILE):
        stop = start + TILE
        here = slice(start, stop)
        back = dot_nn(behind_logit_ref[here, :stop], query_ref[:stop]) * scale
        back_ref[here] = back.astype(bf16)
        back = dot_nn(behind_win_ref[here, :stop], grad_ref[:stop])
        back_ref[span + start : span + stop] = back.astype(bf16)


def own_body(
    behind_logit_ref, own_logit_ref, own_win_ref, halo_ref, query_ref, key_ref, grad_ref,
    gq_ref, gk_ref, gv_ref,
):
    span = query_ref.shape[0]
    scale = 1.0 / math.sqrt(DH)
    for start in range(0, span, TILE):
        stop = start + TILE
        here = slice(start, stop)
        result = dot_tn(halo_ref[start:span], behind_logit_ref[start:, here])
        result = result + dot_tn(key_ref[:stop], own_logit_ref[:stop, here])
        gq_ref[here] = (jnp.transpose(result) * scale).astype(bf16)
        gk_ref[here] = dot_nn(own_logit_ref[here, start:], query_ref[start:]) * scale
        gv_ref[here] = dot_nn(own_win_ref[here, start:], grad_ref[start:])


def settle_body(gk_ref, gv_ref, back_ref, gk_out, gv_out, done_ref):
    span = gk_ref.shape[0]
    gk_out[...] = (gk_ref[...] + back_ref[:span].astype(f32)).astype(bf16)
    gv_out[...] = (gv_ref[...] + back_ref[span:].astype(f32)).astype(bf16)
    done_ref[...] = jnp.zeros_like(done_ref)


def local(
    query_lin, key_lin, value_lin, norm_gain, grad_normed, query_win, key_win, value_win, grad_win
):
    tokens, width = query_lin.shape
    blocks, heads = lax.axis_size("ctx"), lax.axis_size("head")
    rows = blocks // ROW
    my_index = lax.axis_index("ctx")
    where = jnp.stack([my_index // ROW, my_index % ROW, my_index]).astype(jnp.int32)
    row_groups = [[row * ROW + col for col in range(ROW)] for row in range(rows)]
    col_groups = [[row * ROW + col for row in range(rows)] for col in range(ROW)]
    gain = norm_gain.reshape(1, width)
    state = (DH, DH)
    block = (tokens, width)
    macs = tokens * DH * DH
    square = tokens * tokens * DH
    size = tokens * DH * 2
    in_smem = pl.BlockSpec(memory_space=pltpu.SMEM)
    in_vmem = pl.BlockSpec(memory_space=pltpu.VMEM)
    in_hbm = pl.BlockSpec(memory_space=pltpu.HBM)
    anywhere = pl.BlockSpec(memory_space=pl.ANY)
    copies = pltpu.SemaphoreType.DMA((ROW,))
    spreading = (pltpu.VMEM(state, bf16), pltpu.SemaphoreType.DMA((max(rows, ROW),)))

    def along_row(value):
        return lax.all_to_all(value, "ctx", 0, 0, axis_index_groups=row_groups)

    def along_col(value):
        return lax.all_to_all(value, "ctx", 0, 0, axis_index_groups=col_groups)

    def row_total(parts, flops, *ahead):
        return kernel_call(
            total_body,
            shaped((rows,) + state, bf16),
            flops,
            16 * DH * DH * 2,
            scratch=spreading,
            specs=[in_vmem] + [anywhere] * len(ahead),
            out_specs=in_hbm,
            ahead=len(ahead),
        )(parts, *ahead)

    def shift(value, steps):
        first, last = max(0, -steps), min(blocks, blocks - steps)
        return lax.ppermute(value, "ctx", [(at, at + steps) for at in range(first, last)])

    warm = kernel_call(warm_body, shaped((8, TILE), f32), LONG, 0, specs=[in_smem])(where)
    own_state = kernel_call(
        state_body,
        shaped((ROW,) + state, bf16),
        2 * macs,
        2 * size + ROW * DH * DH * 2,
        specs=[in_vmem] * 2 + [anywhere],
        ahead=1,
    )(key_lin, value_lin, warm)
    parts = along_row(own_state)
    row_sum = row_total(parts, 8 * DH * DH)
    halo_pack = kernel_call(
        pack_body,
        shaped((2 * tokens, width), bf16),
        0,
        4 * size,
        specs=[in_vmem] * 2 + [anywhere],
        ahead=1,
    )(key_win, value_win, row_sum)
    halo = shift(halo_pack, 1)
    inner, scaled = kernel_call(
        inner_body,
        (shaped(block, f32), shaped(block, f32)),
        2.5 * square,
        8 * size,
        specs=[in_vmem] * 5 + [anywhere],
        ahead=1,
    )(query_lin, key_lin, value_lin, grad_normed, gain, row_sum)
    row_parts = along_col(row_sum)
    lin_out, prior, sums = kernel_call(
        normed_body,
        (shaped(block, f32), shaped(state, f32), shaped((heads, 8, TILE), f32)),
        4 * macs,
        8 * size,
        scratch=(pltpu.VMEM((8, TILE), f32), pltpu.SemaphoreType.DMA((heads,))),
        specs=[in_smem] + [in_vmem] * 5,
        out_specs=(in_vmem, in_vmem, in_hbm),
    )(where, row_parts, parts, inner, query_lin, scaled)
    flat = shaped((tokens, tokens), bf16)
    back, behind_logit, own_logit, own_win = kernel_call(
        window_body,
        (shaped((2 * tokens, width), bf16), flat, flat, flat),
        8 * square,
        20 * size,
        tokens * tokens,
        (pltpu.VMEM((tokens, tokens), bf16),),
        16,
        [in_smem] + [in_vmem] * 5 + [anywhere],
        ahead=1,
    )(where, query_win, key_win, value_win, grad_win, halo, sums)
    gq_win, gk_own, gv_own = kernel_call(
        own_body,
        (shaped(block, bf16), shaped(block, f32), shaped(block, f32)),
        5 * square,
        20 * size,
        specs=[in_vmem] * 7,
    )(behind_logit, own_logit, own_win, halo, query_win, key_win, grad_win)
    all_sums = lax.all_to_all(sums, "head", 0, 0)
    returned = shift(back, -1)
    probs, kept = kernel_call(
        probs_body,
        (shaped((tokens, tokens), bf16), shaped((2 * tokens, width), bf16)),
        LONG,
        8 * size,
        specs=[in_vmem] * 3 + [anywhere],
        ahead=1,
    )(query_lin, key_lin, value_lin, sums)
    grad_out, later_state = kernel_call(
        functools.partial(grad_out_body, width=float(width * heads)),
        (shaped(block, bf16), shaped((ROW,) + state, bf16)),
        2 * macs,
        8 * size,
        specs=[in_vmem] * 4 + [anywhere] * 3,
        ahead=3,
    )(all_sums, lin_out, scaled, query_lin, returned, probs, gk_own)
    later_parts = along_row(later_state)
    later_sum = row_total(later_parts, 8 * DH * DH)
    gq_lin, gk_part, gv_part = kernel_call(
        mixed_body,
        (shaped(block, bf16), shaped(block, f32), shaped(block, f32)),
        5 * square,
        10 * size,
        specs=[in_vmem] * 5 + [anywhere],
        ahead=1,
    )(grad_out, query_lin, kept, probs, prior, later_sum)
    later_rows = along_col(later_sum)
    gk_win, gv_win, settled = kernel_call(
        settle_body,
        (shaped(block, bf16), shaped(block, bf16), shaped((8, TILE), f32)),
        tokens * DH,
        8 * size,
        specs=[in_vmem] * 3 + [anywhere],
        ahead=1,
    )(gk_own, gv_own, returned, later_sum)
    gk_lin, gv_lin = kernel_call(
        closing_body,
        (shaped(block, bf16),) * 2,
        8 * macs,
        8 * size,
        scratch=(pltpu.VMEM(block, bf16), pltpu.VMEM(block, bf16), copies),
        specs=[in_smem] + [in_vmem] * 5 + [anywhere],
        out_specs=(in_hbm, in_hbm),
        ahead=1,
    )(where, later_rows, later_parts, gk_part, gv_part, kept, settled)
    return gq_lin, gk_lin, gv_lin, gq_win, gk_win, gv_win


def solution(mesh):
    placed = P("ctx", "head")
    return jax.shard_map(
        local,
        mesh=mesh,
        in_specs=(placed, placed, placed, P("head")) + (placed,) * 5,
        out_specs=(placed,) * 6,
        check_vma=False,
    )
```

```python
import functools
import math

import jax
import jax.numpy as jnp
from jax import lax
from jax.experimental import pallas as pl
from jax.experimental.pallas import tpu as pltpu
from jax.sharding import PartitionSpec as P

DH = 128
WINDOW = 512
TILE = 128
ROW = 8
NORM_EPS = 1e-06
HIDDEN = -1e30
LONG = 4e9

f32 = jnp.float32
bf16 = jnp.bfloat16


def dot(left, right, dims):
    return lax.dot_general(left, right, (dims, ((), ())), preferred_element_type=f32)


def dot_nn(left, right):
    return dot(left, right, ((1,), (0,)))


def dot_nt(left, right):
    return dot(left, right, ((1,), (1,)))


def dot_tn(left, right):
    return dot(left, right, ((0,), (0,)))


def halves(value):
    high = value.astype(bf16)
    return high, (value - high.astype(f32)).astype(bf16)


def kernel_call(
    body, outs, flops, moved, exps=0, scratch=(), limit=12, specs=None, out_specs=None, ahead=0
):
    def run(*refs):
        inputs = len(specs)
        body(*refs[: inputs - ahead], *refs[inputs:])

    return pl.pallas_call(
        run if ahead else body,
        name=getattr(body, "func", body).__name__,
        out_shape=outs,
        scratch_shapes=list(scratch),
        compiler_params=pltpu.CompilerParams(vmem_limit_bytes=limit << 20),
        cost_estimate=pl.CostEstimate(
            flops=int(flops), bytes_accessed=int(moved), transcendentals=int(exps)
        ),
        **({"in_specs": specs} if specs else {}),
        **({"out_specs": out_specs} if out_specs else {}),
    )


def shaped(shape, dtype):
    return jax.ShapeDtypeStruct(shape, dtype)


def diagonal_tiles():
    rows = lax.broadcasted_iota(jnp.int32, (TILE, TILE), 0)
    cols = lax.broadcasted_iota(jnp.int32, (TILE, TILE), 1)
    return rows <= cols, rows >= cols


def chosen_body(where_ref, out_ref):
    row, col, index = where_ref[0], where_ref[1], where_ref[2]
    place = lax.broadcasted_iota(jnp.int32, (ROW, TILE), 0)
    for group, wanted in enumerate((place < row, place < col, place > row, place > col)):
        out_ref[group * ROW : (group + 1) * ROW] = jnp.where(wanted, 1.0, 0.0)
    out_ref[4 * ROW :] = jnp.where(place >= index * ROW, 1.0, 0.0)


def state_body(key_ref, value_ref, out_ref):
    state = dot_tn(key_ref[...], value_ref[...]).astype(bf16)
    for place in range(out_ref.shape[0]):
        out_ref[place] = state


def spread(value, near, far, sent):
    near[...] = value
    copies = [
        pltpu.make_async_copy(near, far.at[place], sent.at[place]) for place in range(far.shape[0])
    ]
    for copy in copies:
        copy.start()
    return copies


def total_body(parts_ref, out_hbm, near, sent):
    total = parts_ref[0].astype(f32)
    for place in range(1, parts_ref.shape[0]):
        total = total + parts_ref[place].astype(f32)
    for copy in spread(total.astype(bf16), near, out_hbm, sent):
        copy.wait()


def pack_body(key_ref, value_ref, out_ref):
    span = key_ref.shape[0]
    out_ref[:span] = key_ref[...]
    out_ref[span:] = value_ref[...]


def chosen_sum(chosen_ref, rows_ref, parts_ref, later):
    total = None
    base = 2 * ROW if later else 0
    for ref, first in ((rows_ref, base), (parts_ref, base + ROW)):
        for place in range(ref.shape[0]):
            wanted = chosen_ref[first + place : first + place + 1, :]
            term = ref[place].astype(f32) * wanted
            total = term if total is None else total + term
    return total


def inner_body(
    query_ref, key_ref, value_ref, grad_ref, gain_ref,
    probs_ref, kept_ref, inner_ref, scaled_ref,
):
    tokens = query_ref.shape[0]
    kept_ref[:tokens] = key_ref[...]
    kept_ref[tokens:] = value_ref[...]
    upper, _ = diagonal_tiles()
    for start in range(0, tokens, TILE):
        stop = start + TILE
        here = slice(start, stop)
        query = query_ref[here]
        edge = jnp.where(upper, dot_nt(key_ref[here], query), 0.0).astype(bf16)
        probs_ref[here, here] = edge
        result = dot_tn(value_ref[here], edge)
        if start:
            probs = dot_nt(key_ref[:start], query).astype(bf16)
            probs_ref[:start, here] = probs
            result = result + dot_tn(value_ref[:start], probs)
        inner_ref[:, here] = result
        scaled_ref[:, here] = jnp.transpose(grad_ref[here].astype(f32) * gain_ref[...])


def normed_body(
    chosen_ref, rows_ref, parts_ref, inner_ref, query_ref, scaled_ref,
    lin_ref, prior_ref, sums_hbm, near, sent,
):
    prior = chosen_sum(chosen_ref, rows_ref, parts_ref, False)
    prior_ref[...] = prior
    high, low = halves(jnp.transpose(prior))
    squares, crosses = [], []
    for start in range(0, query_ref.shape[0], TILE):
        here = slice(start, start + TILE)
        query = query_ref[here]
        lin_out = inner_ref[:, here] + dot_nt(high, query) + dot_nt(low, query)
        lin_ref[:, here] = lin_out
        squares.append(jnp.sum(lin_out * lin_out, axis=0, keepdims=True))
        crosses.append(jnp.sum(scaled_ref[:, here] * lin_out, axis=0, keepdims=True))
    for copy in spread(jnp.concatenate(squares + crosses, 0), near, sums_hbm, sent):
        copy.wait()


def grad_out_body(sums_ref, lin_ref, scaled_ref, query_ref, out_ref, state_ref, *, width):
    total = sums_ref[0]
    for place in range(1, sums_ref.shape[0]):
        total = total + sums_ref[place]
    groups = total.shape[0] // 2
    inverse = 1.0 / jnp.sqrt(total[:groups] / width + NORM_EPS)
    weight = total[groups:] * inverse * inverse * inverse / width
    for group in range(groups):
        tokens = slice(group * TILE, (group + 1) * TILE)
        here = slice(group, group + 1)
        grad_out = scaled_ref[:, tokens] * inverse[here] - lin_ref[:, tokens] * weight[here]
        out_ref[:, tokens] = grad_out.astype(bf16)
    state = jnp.transpose(dot_nn(out_ref[...], query_ref[...])).astype(bf16)
    for place in range(state_ref.shape[0]):
        state_ref[place] = state


def mixed_body(
    turned_ref, query_ref, kept_ref, probs_ref, prior_ref, gq_ref, gk_ref, gv_ref, grad_ref,
):
    tokens = query_ref.shape[0]
    for start in range(0, tokens, TILE):
        here = slice(start, start + TILE)
        grad_ref[here] = jnp.transpose(turned_ref[:, here].astype(f32)).astype(bf16)
    upper, lower = diagonal_tiles()
    high, low = halves(prior_ref[...])
    for start in range(0, tokens, TILE):
        stop = start + TILE
        here = slice(start, stop)
        grad, query = grad_ref[here], query_ref[here]
        key, value = kept_ref[here], kept_ref[tokens + start : tokens + stop]
        mix = jnp.where(lower, dot_nt(grad, value), 0.0).astype(bf16)
        result = dot_nn(mix, key) + dot_nt(grad, high) + dot_nt(grad, low)
        if start:
            mix = dot_nt(grad, kept_ref[tokens : tokens + start]).astype(bf16)
            result = result + dot_nn(mix, kept_ref[:start])
        gq_ref[here] = result.astype(bf16)
        mix = jnp.where(upper, dot_nt(value, grad), 0.0).astype(bf16)
        key_part = dot_nn(mix, query)
        if stop < tokens:
            mix = dot_nt(value, grad_ref[stop:]).astype(bf16)
            key_part = key_part + dot_nn(mix, query_ref[stop:])
        gk_ref[here] = key_part
        gv_ref[here] = dot_nn(probs_ref[here, start:], grad_ref[start:])


def closing_body(
    chosen_ref, rows_ref, parts_ref, gk_part_ref, gv_part_ref, kept_ref,
    gk_hbm, gv_hbm, gk_ref, gv_ref, sent,
):
    high, low = halves(chosen_sum(chosen_ref, rows_ref, parts_ref, True))
    copies = []
    tokens = gk_ref.shape[0]
    for start in range(0, tokens, 2 * TILE):
        here = pl.ds(start, 2 * TILE)
        key, value = kept_ref[here], kept_ref[pl.ds(tokens + start, 2 * TILE)]
        gk_ref[here] = (gk_part_ref[here] + dot_nt(value, high) + dot_nt(value, low)).astype(bf16)
        gv_ref[here] = (gv_part_ref[here] + dot_nn(key, high) + dot_nn(key, low)).astype(bf16)
        for near, far in ((gk_ref, gk_hbm), (gv_ref, gv_hbm)):
            copy = pltpu.make_async_copy(near.at[here], far.at[here], sent.at[len(copies)])
            copy.start()
            copies.append(copy)
    for copy in copies:
        copy.wait()


def window_body(
    chosen_ref, query_ref, key_ref, value_ref, grad_ref, halo_ref,
    back_ref, behind_logit_ref, own_logit_ref, own_win_ref, behind_win_ref,
):
    span = query_ref.shape[0]
    scale = 1.0 / math.sqrt(DH)
    first = chosen_ref[4 * ROW : 4 * ROW + 1, :] > 0.5
    upper, _ = diagonal_tiles()
    for start in range(0, span, TILE):
        stop = start + TILE
        here = slice(start, stop)
        query, grad = query_ref[here], grad_ref[here]
        behind = dot_nt(halo_ref[start:span], query)
        edge = jnp.where(upper, HIDDEN, behind[:TILE])
        behind = jnp.concatenate([edge, behind[TILE:]], 0) if stop < span else edge
        behind = jnp.where(first, HIDDEN, behind)
        own = dot_nt(key_ref[:stop], query)
        edge = jnp.where(upper, own[start:], HIDDEN)
        own = jnp.concatenate([own[:start], edge], 0) if start else edge
        peak = jnp.maximum(
            jnp.max(behind, axis=0, keepdims=True), jnp.max(own, axis=0, keepdims=True)
        )
        behind = jnp.exp((behind - peak) * scale)
        own = jnp.exp((own - peak) * scale)
        total = jnp.sum(behind, axis=0, keepdims=True) + jnp.sum(own, axis=0, keepdims=True)
        inverse = 1.0 / total
        behind, own = behind * inverse, own * inverse
        behind_win, own_win = behind.astype(bf16), own.astype(bf16)
        behind_grad = dot_nt(halo_ref[span + start :], grad)
        own_grad = dot_nt(value_ref[:stop], grad)
        delta = jnp.sum(behind_win.astype(f32) * behind_grad, axis=0, keepdims=True) + jnp.sum(
            own_win.astype(f32) * own_grad, axis=0, keepdims=True
        )
        behind_win_ref[start:, here] = behind_win
        own_win_ref[:stop, here] = own_win
        behind_logit_ref[start:, here] = (behind * (behind_grad - delta)).astype(bf16)
        own_logit_ref[:stop, here] = (own * (own_grad - delta)).astype(bf16)
    for start in range(0, span, TILE):
        stop = start + TILE
        here = slice(start, stop)
        back = dot_nn(behind_logit_ref[here, :stop], query_ref[:stop]) * scale
        back_ref[here] = back.astype(bf16)
        back = dot_nn(behind_win_ref[here, :stop], grad_ref[:stop])
        back_ref[span + start : span + stop] = back.astype(bf16)


def own_body(
    behind_logit_ref, own_logit_ref, own_win_ref, halo_ref, query_ref, key_ref, grad_ref,
    gq_ref, gk_ref, gv_ref,
):
    span = query_ref.shape[0]
    scale = 1.0 / math.sqrt(DH)
    for start in range(0, span, TILE):
        stop = start + TILE
        here = slice(start, stop)
        result = dot_tn(halo_ref[start:span], behind_logit_ref[start:, here])
        result = result + dot_tn(key_ref[:stop], own_logit_ref[:stop, here])
        gq_ref[here] = (jnp.transpose(result) * scale).astype(bf16)
        gk_ref[here] = dot_nn(own_logit_ref[here, start:], query_ref[start:]) * scale
        gv_ref[here] = dot_nn(own_win_ref[here, start:], grad_ref[start:])


def settle_body(gk_ref, gv_ref, back_ref, gk_out, gv_out, done_ref):
    span = gk_ref.shape[0]
    gk_out[...] = (gk_ref[...] + back_ref[:span].astype(f32)).astype(bf16)
    gv_out[...] = (gv_ref[...] + back_ref[span:].astype(f32)).astype(bf16)
    done_ref[...] = jnp.zeros_like(done_ref)


def local(
    query_lin, key_lin, value_lin, norm_gain, grad_normed, query_win, key_win, value_win, grad_win
):
    tokens, width = query_lin.shape
    blocks, heads = lax.axis_size("ctx"), lax.axis_size("head")
    rows = blocks // ROW
    my_index = lax.axis_index("ctx")
    where = jnp.stack([my_index // ROW, my_index % ROW, my_index]).astype(jnp.int32)
    row_groups = [[row * ROW + col for col in range(ROW)] for row in range(rows)]
    col_groups = [[row * ROW + col for row in range(rows)] for col in range(ROW)]
    gain = norm_gain.reshape(1, width)
    state = (DH, DH)
    block = (tokens, width)
    macs = tokens * DH * DH
    square = tokens * tokens * DH
    size = tokens * DH * 2
    in_vmem = pl.BlockSpec(memory_space=pltpu.VMEM)
    in_hbm = pl.BlockSpec(memory_space=pltpu.HBM)
    anywhere = pl.BlockSpec(memory_space=pl.ANY)
    copies = pltpu.SemaphoreType.DMA((ROW,))
    spreading = (pltpu.VMEM(state, bf16), pltpu.SemaphoreType.DMA((max(rows, ROW),)))

    def along_row(value):
        return lax.all_to_all(value, "ctx", 0, 0, axis_index_groups=row_groups)

    def along_col(value):
        return lax.all_to_all(value, "ctx", 0, 0, axis_index_groups=col_groups)

    def row_total(parts, flops, *ahead):
        return kernel_call(
            total_body,
            shaped((rows,) + state, bf16),
            flops,
            16 * DH * DH * 2,
            scratch=spreading,
            specs=[in_vmem] + [anywhere] * len(ahead),
            out_specs=in_hbm,
            ahead=len(ahead),
        )(parts, *ahead)

    def shift(value, steps):
        first, last = max(0, -steps), min(blocks, blocks - steps)
        return lax.ppermute(value, "ctx", [(at, at + steps) for at in range(first, last)])

    chosen = kernel_call(
        chosen_body,
        shaped((5 * ROW, TILE), f32),
        LONG,
        0,
        specs=[pl.BlockSpec(memory_space=pltpu.SMEM)],
    )(where)
    own_state = kernel_call(
        state_body,
        shaped((ROW,) + state, bf16),
        2 * macs,
        2 * size + ROW * DH * DH * 2,
        specs=[in_vmem] * 2 + [anywhere],
        ahead=1,
    )(key_lin, value_lin, chosen)
    parts = along_row(own_state)
    row_sum = row_total(parts, 8 * DH * DH)
    halo_pack = kernel_call(
        pack_body,
        shaped((2 * tokens, width), bf16),
        0,
        4 * size,
        specs=[in_vmem] * 2 + [anywhere],
        ahead=1,
    )(key_win, value_win, row_sum)
    halo = shift(halo_pack, 1)
    turned = (width, tokens)
    probs, kept, inner, scaled = kernel_call(
        inner_body,
        (
            shaped((tokens, tokens), bf16),
            shaped((2 * tokens, width), bf16),
            shaped(turned, f32),
            shaped(turned, f32),
        ),
        2.5 * square,
        8 * size,
        specs=[in_vmem] * 5 + [anywhere],
        ahead=1,
    )(query_lin, key_lin, value_lin, grad_normed, gain, row_sum)
    row_parts = along_col(row_sum)
    lin_out, prior, sums = kernel_call(
        normed_body,
        (shaped(turned, f32), shaped(state, f32), shaped((heads, 8, TILE), f32)),
        4 * macs,
        8 * size,
        scratch=(pltpu.VMEM((8, TILE), f32), pltpu.SemaphoreType.DMA((heads,))),
        specs=[in_vmem] + [in_vmem] * 5,
        out_specs=(in_vmem, in_vmem, in_hbm),
    )(chosen, row_parts, parts, inner, query_lin, scaled)
    flat = shaped((tokens, tokens), bf16)
    back, behind_logit, own_logit, own_win = kernel_call(
        window_body,
        (shaped((2 * tokens, width), bf16), flat, flat, flat),
        8 * square,
        20 * size,
        tokens * tokens,
        (pltpu.VMEM((tokens, tokens), bf16),),
        16,
        [in_vmem] + [in_vmem] * 5 + [anywhere],
        ahead=1,
    )(chosen, query_win, key_win, value_win, grad_win, halo, sums)
    gq_win, gk_own, gv_own = kernel_call(
        own_body,
        (shaped(block, bf16), shaped(block, f32), shaped(block, f32)),
        LONG,
        20 * size,
        specs=[in_vmem] * 7 + [anywhere],
        ahead=1,
    )(behind_logit, own_logit, own_win, halo, query_win, key_win, grad_win, sums)
    all_sums = lax.all_to_all(sums, "head", 0, 0)
    returned = shift(back, -1)
    grad_out, later_state = kernel_call(
        functools.partial(grad_out_body, width=float(width * heads)),
        (shaped(turned, bf16), shaped((ROW,) + state, bf16)),
        2 * macs,
        8 * size,
        specs=[in_vmem] * 4 + [anywhere] * 2,
        ahead=2,
    )(all_sums, lin_out, scaled, query_lin, returned, gk_own)
    later_parts = along_row(later_state)
    later_sum = row_total(later_parts, 8 * DH * DH)
    gq_lin, gk_part, gv_part = kernel_call(
        mixed_body,
        (shaped(block, bf16), shaped(block, f32), shaped(block, f32)),
        5 * square,
        10 * size,
        scratch=(pltpu.VMEM(block, bf16),),
        specs=[in_vmem] * 5 + [anywhere],
        ahead=1,
    )(grad_out, query_lin, kept, probs, prior, later_sum)
    later_rows = along_col(later_sum)
    gk_win, gv_win, settled = kernel_call(
        settle_body,
        (shaped(block, bf16), shaped(block, bf16), shaped((8, TILE), f32)),
        tokens * DH,
        8 * size,
        specs=[in_vmem] * 3 + [anywhere],
        ahead=1,
    )(gk_own, gv_own, returned, later_sum)
    gk_lin, gv_lin = kernel_call(
        closing_body,
        (shaped(block, bf16),) * 2,
        8 * macs,
        8 * size,
        scratch=(pltpu.VMEM(block, bf16), pltpu.VMEM(block, bf16), copies),
        specs=[in_vmem] + [in_vmem] * 5 + [anywhere],
        out_specs=(in_hbm, in_hbm),
        ahead=1,
    )(chosen, later_rows, later_parts, gk_part, gv_part, kept, settled)
    return gq_lin, gk_lin, gv_lin, gq_win, gk_win, gv_win


def solution(mesh):
    placed = P("ctx", "head")
    return jax.shard_map(
        local,
        mesh=mesh,
        in_specs=(placed, placed, placed, P("head")) + (placed,) * 5,
        out_specs=(placed,) * 6,
        check_vma=False,
    )
```

```python
import functools
import math

import jax
import jax.numpy as jnp
from jax import lax
from jax.experimental import pallas as pl
from jax.experimental.pallas import tpu as pltpu
from jax.sharding import PartitionSpec as P

DH = 128
WINDOW = 512
TILE = 128
ROW = 8
NORM_EPS = 1e-06
HIDDEN = -1e30
LONG = 4e9

f32 = jnp.float32
bf16 = jnp.bfloat16


def dot(left, right, dims):
    return lax.dot_general(left, right, (dims, ((), ())), preferred_element_type=f32)


def dot_nn(left, right):
    return dot(left, right, ((1,), (0,)))


def dot_nt(left, right):
    return dot(left, right, ((1,), (1,)))


def dot_tn(left, right):
    return dot(left, right, ((0,), (0,)))


def halves(value):
    high = value.astype(bf16)
    return high, (value - high.astype(f32)).astype(bf16)


def kernel_call(
    body, outs, flops, moved, exps=0, scratch=(), limit=12, specs=None, out_specs=None, ahead=0
):
    def run(*refs):
        inputs = len(specs)
        body(*refs[: inputs - ahead], *refs[inputs:])

    return pl.pallas_call(
        run if ahead else body,
        name=getattr(body, "func", body).__name__,
        out_shape=outs,
        scratch_shapes=list(scratch),
        compiler_params=pltpu.CompilerParams(vmem_limit_bytes=limit << 20),
        cost_estimate=pl.CostEstimate(
            flops=int(flops), bytes_accessed=int(moved), transcendentals=int(exps)
        ),
        **({"in_specs": specs} if specs else {}),
        **({"out_specs": out_specs} if out_specs else {}),
    )


def shaped(shape, dtype):
    return jax.ShapeDtypeStruct(shape, dtype)


def diagonal_tiles():
    rows = lax.broadcasted_iota(jnp.int32, (TILE, TILE), 0)
    cols = lax.broadcasted_iota(jnp.int32, (TILE, TILE), 1)
    return rows <= cols, rows >= cols


def chosen_body(where_ref, out_ref):
    row, col, index = where_ref[0], where_ref[1], where_ref[2]
    place = lax.broadcasted_iota(jnp.int32, (ROW, TILE), 0)
    for group, wanted in enumerate((place < row, place < col, place > row, place > col)):
        out_ref[group * ROW : (group + 1) * ROW] = jnp.where(wanted, 1.0, 0.0)
    out_ref[4 * ROW :] = jnp.where(place >= index * ROW, 1.0, 0.0)


def state_body(key_ref, value_ref, out_ref):
    state = dot_tn(key_ref[...], value_ref[...]).astype(bf16)
    for place in range(out_ref.shape[0]):
        out_ref[place] = state


def spread(value, near, far, sent):
    near[...] = value
    copies = [
        pltpu.make_async_copy(near, far.at[place], sent.at[place]) for place in range(far.shape[0])
    ]
    for copy in copies:
        copy.start()
    return copies


def total_body(parts_ref, out_hbm, near, sent):
    total = parts_ref[0].astype(f32)
    for place in range(1, parts_ref.shape[0]):
        total = total + parts_ref[place].astype(f32)
    for copy in spread(total.astype(bf16), near, out_hbm, sent):
        copy.wait()


def pack_body(key_ref, value_ref, out_ref):
    span = key_ref.shape[0]
    out_ref[:span] = key_ref[...]
    out_ref[span:] = value_ref[...]


def chosen_sum(chosen_ref, group, ref):
    total = None
    for place in range(ref.shape[0]):
        first = group * ROW + place
        term = ref[place].astype(f32) * chosen_ref[first : first + 1, :]
        total = term if total is None else total + term
    return total


def twice(value):
    return jnp.concatenate([value, value], 1)


def inner_body(
    chosen_ref, parts_ref, query_ref, key_ref, value_ref, grad_ref, gain_ref,
    probs_ref, kept_ref, inner_ref, scaled_ref, base_ref,
):
    base_ref[...] = chosen_sum(chosen_ref, 1, parts_ref)
    tokens = query_ref.shape[0]
    kept_ref[:tokens] = key_ref[...]
    kept_ref[tokens:] = value_ref[...]
    upper, _ = diagonal_tiles()
    for start in range(0, tokens, TILE):
        stop = start + TILE
        here = slice(start, stop)
        query = query_ref[here]
        edge = jnp.where(upper, dot_nt(key_ref[here], query), 0.0).astype(bf16)
        probs_ref[here, here] = edge
        result = dot_tn(value_ref[here], edge)
        if start:
            probs = dot_nt(key_ref[:start], query).astype(bf16)
            probs_ref[:start, here] = probs
            result = result + dot_tn(value_ref[:start], probs)
        inner_ref[:, here] = result
        scaled_ref[:, here] = jnp.transpose(grad_ref[here].astype(f32) * gain_ref[...])


def normed_body(
    chosen_ref, rows_ref, base_ref, inner_ref, query_ref, scaled_ref,
    lin_ref, prior_ref, sums_hbm, near, sent,
):
    prior = base_ref[...] + chosen_sum(chosen_ref, 0, rows_ref)
    prior_ref[...] = prior
    both = jnp.concatenate(halves(jnp.transpose(prior)), 1)
    squares, crosses = [], []
    for start in range(0, query_ref.shape[0], TILE):
        here = slice(start, start + TILE)
        lin_out = inner_ref[:, here] + dot_nt(both, twice(query_ref[here]))
        lin_ref[:, here] = lin_out
        squares.append(jnp.sum(lin_out * lin_out, axis=0, keepdims=True))
        crosses.append(jnp.sum(scaled_ref[:, here] * lin_out, axis=0, keepdims=True))
    for copy in spread(jnp.concatenate(squares + crosses, 0), near, sums_hbm, sent):
        copy.wait()


def grad_out_body(sums_ref, lin_ref, scaled_ref, query_ref, out_ref, state_ref, *, width):
    total = sums_ref[0]
    for place in range(1, sums_ref.shape[0]):
        total = total + sums_ref[place]
    groups = total.shape[0] // 2
    inverse = 1.0 / jnp.sqrt(total[:groups] / width + NORM_EPS)
    weight = total[groups:] * inverse * inverse * inverse / width
    for group in range(groups):
        tokens = slice(group * TILE, (group + 1) * TILE)
        here = slice(group, group + 1)
        grad_out = scaled_ref[:, tokens] * inverse[here] - lin_ref[:, tokens] * weight[here]
        out_ref[:, tokens] = grad_out.astype(bf16)
    state = jnp.transpose(dot_nn(out_ref[...], query_ref[...])).astype(bf16)
    for place in range(state_ref.shape[0]):
        state_ref[place] = state


def mixed_body(
    chosen_ref, parts_ref, turned_ref, query_ref, kept_ref, probs_ref, prior_ref,
    gq_ref, gk_ref, gv_ref, base_ref, grad_ref,
):
    base_ref[...] = chosen_sum(chosen_ref, 3, parts_ref)
    tokens = query_ref.shape[0]
    for start in range(0, tokens, TILE):
        here = slice(start, start + TILE)
        grad_ref[here] = jnp.transpose(turned_ref[:, here].astype(f32)).astype(bf16)
    upper, lower = diagonal_tiles()
    high, low = halves(prior_ref[...])
    for start in range(0, tokens, TILE):
        stop = start + TILE
        here = slice(start, stop)
        grad, query = grad_ref[here], query_ref[here]
        key, value = kept_ref[here], kept_ref[tokens + start : tokens + stop]
        mix = jnp.where(lower, dot_nt(grad, value), 0.0).astype(bf16)
        result = dot_nn(mix, key) + dot_nt(grad, high) + dot_nt(grad, low)
        if start:
            mix = dot_nt(grad, kept_ref[tokens : tokens + start]).astype(bf16)
            result = result + dot_nn(mix, kept_ref[:start])
        gq_ref[here] = result.astype(bf16)
        mix = jnp.where(upper, dot_nt(value, grad), 0.0).astype(bf16)
        key_part = dot_nn(mix, query)
        if stop < tokens:
            mix = dot_nt(value, grad_ref[stop:]).astype(bf16)
            key_part = key_part + dot_nn(mix, query_ref[stop:])
        gk_ref[here] = key_part
        gv_ref[here] = dot_nn(probs_ref[here, start:], grad_ref[start:])


def closing_body(
    chosen_ref, rows_ref, base_ref, gk_part_ref, gv_part_ref, kept_ref,
    gk_hbm, gv_hbm, gk_ref, gv_ref, sent,
):
    high, low = halves(base_ref[...] + chosen_sum(chosen_ref, 2, rows_ref))
    wide, tall = jnp.concatenate([high, low], 1), jnp.concatenate([high, low], 0)
    copies = []
    tokens = gk_ref.shape[0]
    for start in range(0, tokens, 2 * TILE):
        here = pl.ds(start, 2 * TILE)
        key, value = kept_ref[here], kept_ref[pl.ds(tokens + start, 2 * TILE)]
        gk_ref[here] = (gk_part_ref[here] + dot_nt(twice(value), wide)).astype(bf16)
        gv_ref[here] = (gv_part_ref[here] + dot_nn(twice(key), tall)).astype(bf16)
        for near, far in ((gk_ref, gk_hbm), (gv_ref, gv_hbm)):
            copy = pltpu.make_async_copy(near.at[here], far.at[here], sent.at[len(copies)])
            copy.start()
            copies.append(copy)
    for copy in copies:
        copy.wait()


def window_body(
    chosen_ref, query_ref, key_ref, value_ref, grad_ref, halo_ref,
    back_ref, behind_logit_ref, own_logit_ref, own_win_ref, behind_win_ref,
):
    span = query_ref.shape[0]
    scale = 1.0 / math.sqrt(DH)
    first = chosen_ref[4 * ROW : 4 * ROW + 1, :] > 0.5
    upper, _ = diagonal_tiles()
    for start in range(0, span, TILE):
        stop = start + TILE
        here = slice(start, stop)
        query, grad = query_ref[here], grad_ref[here]
        behind = dot_nt(halo_ref[start:span], query) * scale
        edge = jnp.where(upper, HIDDEN, behind[:TILE])
        behind = jnp.concatenate([edge, behind[TILE:]], 0) if stop < span else edge
        behind = jnp.where(first, HIDDEN, behind)
        own = dot_nt(key_ref[:stop], query) * scale
        edge = jnp.where(upper, own[start:], HIDDEN)
        own = jnp.concatenate([own[:start], edge], 0) if start else edge
        peak = jnp.maximum(
            jnp.max(behind, axis=0, keepdims=True), jnp.max(own, axis=0, keepdims=True)
        )
        behind = jnp.exp(behind - peak)
        own = jnp.exp(own - peak)
        total = jnp.sum(behind, axis=0, keepdims=True) + jnp.sum(own, axis=0, keepdims=True)
        behind, own = behind / total, own / total
        behind_win, own_win = behind.astype(bf16), own.astype(bf16)
        behind_grad = dot_nt(halo_ref[span + start :], grad)
        own_grad = dot_nt(value_ref[:stop], grad)
        delta = jnp.sum(behind_win.astype(f32) * behind_grad, axis=0, keepdims=True) + jnp.sum(
            own_win.astype(f32) * own_grad, axis=0, keepdims=True
        )
        behind_win_ref[start:, here] = behind_win
        own_win_ref[:stop, here] = own_win
        behind_logit_ref[start:, here] = (behind * (behind_grad - delta)).astype(bf16)
        own_logit_ref[:stop, here] = (own * (own_grad - delta)).astype(bf16)
    for start in range(0, span, TILE):
        stop = start + TILE
        here = slice(start, stop)
        back = dot_nn(behind_logit_ref[here, :stop], query_ref[:stop]) * scale
        back_ref[here] = back.astype(bf16)
        back = dot_nn(behind_win_ref[here, :stop], grad_ref[:stop])
        back_ref[span + start : span + stop] = back.astype(bf16)


def own_body(
    behind_logit_ref, own_logit_ref, own_win_ref, halo_ref, query_ref, key_ref, grad_ref,
    gq_ref, gk_ref, gv_ref,
):
    span = query_ref.shape[0]
    scale = 1.0 / math.sqrt(DH)
    for start in range(0, span, TILE):
        stop = start + TILE
        here = slice(start, stop)
        result = dot_tn(halo_ref[start:span], behind_logit_ref[start:, here])
        result = result + dot_tn(key_ref[:stop], own_logit_ref[:stop, here])
        gq_ref[here] = (jnp.transpose(result) * scale).astype(bf16)
        gk_ref[here] = dot_nn(own_logit_ref[here, start:], query_ref[start:]) * scale
        gv_ref[here] = dot_nn(own_win_ref[here, start:], grad_ref[start:])


def settle_body(gk_ref, gv_ref, back_ref, gk_out, gv_out, done_ref):
    span = gk_ref.shape[0]
    gk_out[...] = (gk_ref[...] + back_ref[:span].astype(f32)).astype(bf16)
    gv_out[...] = (gv_ref[...] + back_ref[span:].astype(f32)).astype(bf16)
    done_ref[...] = jnp.zeros_like(done_ref)


def local(
    query_lin, key_lin, value_lin, norm_gain, grad_normed, query_win, key_win, value_win, grad_win
):
    tokens, width = query_lin.shape
    blocks, heads = lax.axis_size("ctx"), lax.axis_size("head")
    rows = blocks // ROW
    my_index = lax.axis_index("ctx")
    where = jnp.stack([my_index // ROW, my_index % ROW, my_index]).astype(jnp.int32)
    row_groups = [[row * ROW + col for col in range(ROW)] for row in range(rows)]
    col_groups = [[row * ROW + col for row in range(rows)] for col in range(ROW)]
    gain = norm_gain.reshape(1, width)
    state = (DH, DH)
    block = (tokens, width)
    macs = tokens * DH * DH
    square = tokens * tokens * DH
    size = tokens * DH * 2
    in_vmem = pl.BlockSpec(memory_space=pltpu.VMEM)
    in_hbm = pl.BlockSpec(memory_space=pltpu.HBM)
    anywhere = pl.BlockSpec(memory_space=pl.ANY)
    copies = pltpu.SemaphoreType.DMA((ROW,))
    spreading = (pltpu.VMEM(state, bf16), pltpu.SemaphoreType.DMA((max(rows, ROW),)))

    def along_row(value):
        return lax.all_to_all(value, "ctx", 0, 0, axis_index_groups=row_groups)

    def along_col(value):
        return lax.all_to_all(value, "ctx", 0, 0, axis_index_groups=col_groups)

    def row_total(parts, flops, *ahead):
        return kernel_call(
            total_body,
            shaped((rows,) + state, bf16),
            flops,
            16 * DH * DH * 2,
            scratch=spreading,
            specs=[in_vmem] + [anywhere] * len(ahead),
            out_specs=in_hbm,
            ahead=len(ahead),
        )(parts, *ahead)

    def shift(value, steps):
        first, last = max(0, -steps), min(blocks, blocks - steps)
        return lax.ppermute(value, "ctx", [(at, at + steps) for at in range(first, last)])

    chosen = kernel_call(
        chosen_body,
        shaped((5 * ROW, TILE), f32),
        LONG,
        0,
        specs=[pl.BlockSpec(memory_space=pltpu.SMEM)],
    )(where)
    own_state = kernel_call(
        state_body,
        shaped((ROW,) + state, bf16),
        2 * macs,
        2 * size + ROW * DH * DH * 2,
        specs=[in_vmem] * 2 + [anywhere],
        ahead=1,
    )(key_lin, value_lin, chosen)
    parts = along_row(own_state)
    row_sum = row_total(parts, 8 * DH * DH)
    halo_pack = kernel_call(
        pack_body,
        shaped((2 * tokens, width), bf16),
        0,
        4 * size,
        specs=[in_vmem] * 2 + [anywhere],
        ahead=1,
    )(key_win, value_win, row_sum)
    halo = shift(halo_pack, 1)
    turned = (width, tokens)
    probs, kept, inner, scaled, base = kernel_call(
        inner_body,
        (
            shaped((tokens, tokens), bf16),
            shaped((2 * tokens, width), bf16),
            shaped(turned, f32),
            shaped(turned, f32),
            shaped(state, f32),
        ),
        2.5 * square,
        8 * size,
        specs=[in_vmem] * 7 + [anywhere],
        ahead=1,
    )(chosen, parts, query_lin, key_lin, value_lin, grad_normed, gain, row_sum)
    row_parts = along_col(row_sum)
    lin_out, prior, sums = kernel_call(
        normed_body,
        (shaped(turned, f32), shaped(state, f32), shaped((heads, 8, TILE), f32)),
        4 * macs,
        8 * size,
        scratch=(pltpu.VMEM((8, TILE), f32), pltpu.SemaphoreType.DMA((heads,))),
        specs=[in_vmem] + [in_vmem] * 5,
        out_specs=(in_vmem, in_vmem, in_hbm),
    )(chosen, row_parts, base, inner, query_lin, scaled)
    flat = shaped((tokens, tokens), bf16)
    back, behind_logit, own_logit, own_win = kernel_call(
        window_body,
        (shaped((2 * tokens, width), bf16), flat, flat, flat),
        8 * square,
        20 * size,
        tokens * tokens,
        (pltpu.VMEM((tokens, tokens), bf16),),
        16,
        [in_vmem] + [in_vmem] * 5 + [anywhere],
        ahead=1,
    )(chosen, query_win, key_win, value_win, grad_win, halo, sums)
    gq_win, gk_own, gv_own = kernel_call(
        own_body,
        (shaped(block, bf16), shaped(block, f32), shaped(block, f32)),
        LONG,
        20 * size,
        specs=[in_vmem] * 7 + [anywhere],
        ahead=1,
    )(behind_logit, own_logit, own_win, halo, query_win, key_win, grad_win, sums)
    all_sums = lax.all_to_all(sums, "head", 0, 0)
    returned = shift(back, -1)
    grad_out, later_state = kernel_call(
        functools.partial(grad_out_body, width=float(width * heads)),
        (shaped(turned, bf16), shaped((ROW,) + state, bf16)),
        2 * macs,
        8 * size,
        specs=[in_vmem] * 4 + [anywhere] * 2,
        ahead=2,
    )(all_sums, lin_out, scaled, query_lin, returned, gk_own)
    later_parts = along_row(later_state)
    later_sum = row_total(later_parts, 8 * DH * DH)
    gq_lin, gk_part, gv_part, later_base = kernel_call(
        mixed_body,
        (shaped(block, bf16), shaped(block, f32), shaped(block, f32), shaped(state, f32)),
        5 * square,
        10 * size,
        scratch=(pltpu.VMEM(block, bf16),),
        specs=[in_vmem] * 7 + [anywhere],
        ahead=1,
    )(chosen, later_parts, grad_out, query_lin, kept, probs, prior, later_sum)
    later_rows = along_col(later_sum)
    gk_win, gv_win, settled = kernel_call(
        settle_body,
        (shaped(block, bf16), shaped(block, bf16), shaped((8, TILE), f32)),
        tokens * DH,
        8 * size,
        specs=[in_vmem] * 3 + [anywhere],
        ahead=1,
    )(gk_own, gv_own, returned, later_sum)
    gk_lin, gv_lin = kernel_call(
        closing_body,
        (shaped(block, bf16),) * 2,
        8 * macs,
        8 * size,
        scratch=(pltpu.VMEM(block, bf16), pltpu.VMEM(block, bf16), copies),
        specs=[in_vmem] + [in_vmem] * 5 + [anywhere],
        out_specs=(in_hbm, in_hbm),
        ahead=1,
    )(chosen, later_rows, later_base, gk_part, gv_part, kept, settled)
    return gq_lin, gk_lin, gv_lin, gq_win, gk_win, gv_win


def solution(mesh):
    placed = P("ctx", "head")
    return jax.shard_map(
        local,
        mesh=mesh,
        in_specs=(placed, placed, placed, P("head")) + (placed,) * 5,
        out_specs=(placed,) * 6,
        check_vma=False,
    )
```

```python
import functools
import math

import jax
import jax.numpy as jnp
from jax import lax
from jax.experimental import pallas as pl
from jax.experimental.pallas import tpu as pltpu
from jax.sharding import PartitionSpec as P

DH = 128
WINDOW = 512
TILE = 128
ROW = 8
NORM_EPS = 1e-06
HIDDEN = -1e30
LONG = 4e9

f32 = jnp.float32
bf16 = jnp.bfloat16


def dot(left, right, dims):
    return lax.dot_general(left, right, (dims, ((), ())), preferred_element_type=f32)


def dot_nn(left, right):
    return dot(left, right, ((1,), (0,)))


def dot_nt(left, right):
    return dot(left, right, ((1,), (1,)))


def dot_tn(left, right):
    return dot(left, right, ((0,), (0,)))


def halves(value):
    high = value.astype(bf16)
    return high, (value - high.astype(f32)).astype(bf16)


def kernel_call(
    body, outs, flops, moved, exps=0, scratch=(), limit=12, specs=None, out_specs=None, ahead=0
):
    def run(*refs):
        inputs = len(specs)
        body(*refs[: inputs - ahead], *refs[inputs:])

    return pl.pallas_call(
        run if ahead else body,
        name=getattr(body, "func", body).__name__,
        out_shape=outs,
        scratch_shapes=list(scratch),
        compiler_params=pltpu.CompilerParams(vmem_limit_bytes=limit << 20),
        cost_estimate=pl.CostEstimate(
            flops=int(flops), bytes_accessed=int(moved), transcendentals=int(exps)
        ),
        **({"in_specs": specs} if specs else {}),
        **({"out_specs": out_specs} if out_specs else {}),
    )


def shaped(shape, dtype):
    return jax.ShapeDtypeStruct(shape, dtype)


def diagonal_tiles():
    rows = lax.broadcasted_iota(jnp.int32, (TILE, TILE), 0)
    cols = lax.broadcasted_iota(jnp.int32, (TILE, TILE), 1)
    return rows <= cols, rows >= cols


def chosen_body(where_ref, out_ref):
    index = where_ref[0]
    row, col = lax.div(index, ROW), lax.rem(index, ROW)
    place = lax.broadcasted_iota(jnp.int32, (ROW, TILE), 0)
    for group, wanted in enumerate((place < row, place < col, place > row, place > col)):
        out_ref[group * ROW : (group + 1) * ROW] = jnp.where(wanted, 1.0, 0.0)
    out_ref[4 * ROW :] = jnp.where(place >= index * ROW, 1.0, 0.0)


def state_body(key_ref, value_ref, out_ref):
    state = dot_tn(key_ref[...], value_ref[...]).astype(bf16)
    for place in range(out_ref.shape[0]):
        out_ref[place] = state


def spread(value, near, far, sent):
    near[...] = value
    copies = [
        pltpu.make_async_copy(near, far.at[place], sent.at[place]) for place in range(far.shape[0])
    ]
    for copy in copies:
        copy.start()
    return copies


def total_body(parts_ref, out_hbm, near, sent):
    total = parts_ref[0].astype(f32)
    for place in range(1, parts_ref.shape[0]):
        total = total + parts_ref[place].astype(f32)
    for copy in spread(total.astype(bf16), near, out_hbm, sent):
        copy.wait()


def pack_body(key_ref, value_ref, out_ref):
    span = key_ref.shape[0]
    out_ref[:span] = key_ref[...]
    out_ref[span:] = value_ref[...]


def chosen_sum(chosen_ref, group, ref):
    total = None
    for place in range(ref.shape[0]):
        first = group * ROW + place
        term = ref[place].astype(f32) * chosen_ref[first : first + 1, :]
        total = term if total is None else total + term
    return total


def twice(value):
    return jnp.concatenate([value, value], 1)


def inner_body(
    chosen_ref, parts_ref, query_ref, key_ref, value_ref, grad_ref, gain_ref,
    probs_ref, kept_ref, inner_ref, scaled_ref, base_ref,
):
    base_ref[...] = chosen_sum(chosen_ref, 1, parts_ref)
    tokens = query_ref.shape[0]
    kept_ref[:tokens] = key_ref[...]
    kept_ref[tokens:] = value_ref[...]
    upper, _ = diagonal_tiles()
    for start in range(0, tokens, TILE):
        stop = start + TILE
        here = slice(start, stop)
        query = query_ref[here]
        edge = jnp.where(upper, dot_nt(key_ref[here], query), 0.0).astype(bf16)
        probs_ref[here, here] = edge
        result = dot_tn(value_ref[here], edge)
        if start:
            probs = dot_nt(key_ref[:start], query).astype(bf16)
            probs_ref[:start, here] = probs
            result = result + dot_tn(value_ref[:start], probs)
        inner_ref[:, here] = result
        scaled_ref[:, here] = jnp.transpose(grad_ref[here].astype(f32) * gain_ref[...])


def normed_body(
    chosen_ref, rows_ref, base_ref, inner_ref, query_ref, scaled_ref,
    lin_ref, prior_ref, sums_hbm, near, sent,
):
    prior = base_ref[...] + chosen_sum(chosen_ref, 0, rows_ref)
    prior_ref[...] = prior
    both = jnp.concatenate(halves(jnp.transpose(prior)), 1)
    squares, crosses = [], []
    for start in range(0, query_ref.shape[0], TILE):
        here = slice(start, start + TILE)
        lin_out = inner_ref[:, here] + dot_nt(both, twice(query_ref[here]))
        lin_ref[:, here] = lin_out
        squares.append(jnp.sum(lin_out * lin_out, axis=0, keepdims=True))
        crosses.append(jnp.sum(scaled_ref[:, here] * lin_out, axis=0, keepdims=True))
    for copy in spread(jnp.concatenate(squares + crosses, 0), near, sums_hbm, sent):
        copy.wait()


def grad_out_body(sums_ref, lin_ref, scaled_ref, query_ref, out_ref, state_ref, *, width):
    total = sums_ref[0]
    for place in range(1, sums_ref.shape[0]):
        total = total + sums_ref[place]
    groups = total.shape[0] // 2
    inverse = 1.0 / jnp.sqrt(total[:groups] / width + NORM_EPS)
    weight = total[groups:] * inverse * inverse * inverse / width
    for group in range(groups):
        tokens = slice(group * TILE, (group + 1) * TILE)
        here = slice(group, group + 1)
        grad_out = scaled_ref[:, tokens] * inverse[here] - lin_ref[:, tokens] * weight[here]
        out_ref[:, tokens] = grad_out.astype(bf16)
    state = jnp.transpose(dot_nn(out_ref[...], query_ref[...])).astype(bf16)
    for place in range(state_ref.shape[0]):
        state_ref[place] = state


def mixed_body(
    chosen_ref, parts_ref, turned_ref, query_ref, kept_ref, probs_ref, prior_ref,
    gq_ref, gk_ref, gv_ref, base_ref, grad_ref,
):
    base_ref[...] = chosen_sum(chosen_ref, 3, parts_ref)
    tokens = query_ref.shape[0]
    for start in range(0, tokens, TILE):
        here = slice(start, start + TILE)
        grad_ref[here] = jnp.transpose(turned_ref[:, here].astype(f32)).astype(bf16)
    upper, lower = diagonal_tiles()
    high, low = halves(prior_ref[...])
    for start in range(0, tokens, TILE):
        stop = start + TILE
        here = slice(start, stop)
        grad, query = grad_ref[here], query_ref[here]
        key, value = kept_ref[here], kept_ref[tokens + start : tokens + stop]
        mix = jnp.where(lower, dot_nt(grad, value), 0.0).astype(bf16)
        result = dot_nn(mix, key) + dot_nt(grad, high) + dot_nt(grad, low)
        if start:
            mix = dot_nt(grad, kept_ref[tokens : tokens + start]).astype(bf16)
            result = result + dot_nn(mix, kept_ref[:start])
        gq_ref[here] = result.astype(bf16)
        mix = jnp.where(upper, dot_nt(value, grad), 0.0).astype(bf16)
        key_part = dot_nn(mix, query)
        if stop < tokens:
            mix = dot_nt(value, grad_ref[stop:]).astype(bf16)
            key_part = key_part + dot_nn(mix, query_ref[stop:])
        gk_ref[here] = key_part
        gv_ref[here] = dot_nn(probs_ref[here, start:], grad_ref[start:])


def closing_body(
    chosen_ref, rows_ref, base_ref, gk_part_ref, gv_part_ref, kept_ref,
    gk_hbm, gv_hbm, gk_ref, gv_ref, sent,
):
    high, low = halves(base_ref[...] + chosen_sum(chosen_ref, 2, rows_ref))
    wide, tall = jnp.concatenate([high, low], 1), jnp.concatenate([high, low], 0)
    copies = []
    tokens = gk_ref.shape[0]
    for start in range(0, tokens, 2 * TILE):
        here = pl.ds(start, 2 * TILE)
        key, value = kept_ref[here], kept_ref[pl.ds(tokens + start, 2 * TILE)]
        gk_ref[here] = (gk_part_ref[here] + dot_nt(twice(value), wide)).astype(bf16)
        gv_ref[here] = (gv_part_ref[here] + dot_nn(twice(key), tall)).astype(bf16)
        for near, far in ((gk_ref, gk_hbm), (gv_ref, gv_hbm)):
            copy = pltpu.make_async_copy(near.at[here], far.at[here], sent.at[len(copies)])
            copy.start()
            copies.append(copy)
    for copy in copies:
        copy.wait()


def window_body(
    chosen_ref, query_ref, key_ref, value_ref, grad_ref, halo_ref,
    back_ref, behind_logit_ref, own_logit_ref, own_win_ref, behind_win_ref,
):
    span = query_ref.shape[0]
    scale = 1.0 / math.sqrt(DH)
    first = chosen_ref[4 * ROW : 4 * ROW + 1, :] > 0.5
    upper, _ = diagonal_tiles()
    for start in range(0, span, TILE):
        stop = start + TILE
        here = slice(start, stop)
        query, grad = query_ref[here], grad_ref[here]
        behind = dot_nt(halo_ref[start:span], query) * scale
        edge = jnp.where(upper, HIDDEN, behind[:TILE])
        behind = jnp.concatenate([edge, behind[TILE:]], 0) if stop < span else edge
        behind = jnp.where(first, HIDDEN, behind)
        own = dot_nt(key_ref[:stop], query) * scale
        edge = jnp.where(upper, own[start:], HIDDEN)
        own = jnp.concatenate([own[:start], edge], 0) if start else edge
        peak = jnp.maximum(
            jnp.max(behind, axis=0, keepdims=True), jnp.max(own, axis=0, keepdims=True)
        )
        behind = jnp.exp(behind - peak)
        own = jnp.exp(own - peak)
        total = jnp.sum(behind, axis=0, keepdims=True) + jnp.sum(own, axis=0, keepdims=True)
        behind, own = behind / total, own / total
        behind_win, own_win = behind.astype(bf16), own.astype(bf16)
        behind_grad = dot_nt(halo_ref[span + start :], grad)
        own_grad = dot_nt(value_ref[:stop], grad)
        delta = jnp.sum(behind_win.astype(f32) * behind_grad, axis=0, keepdims=True) + jnp.sum(
            own_win.astype(f32) * own_grad, axis=0, keepdims=True
        )
        behind_win_ref[start:, here] = behind_win
        own_win_ref[:stop, here] = own_win
        behind_logit_ref[start:, here] = (behind * (behind_grad - delta)).astype(bf16)
        own_logit_ref[:stop, here] = (own * (own_grad - delta)).astype(bf16)
    for start in range(0, span, TILE):
        stop = start + TILE
        here = slice(start, stop)
        back = dot_nn(behind_logit_ref[here, :stop], query_ref[:stop]) * scale
        back_ref[here] = back.astype(bf16)
        back = dot_nn(behind_win_ref[here, :stop], grad_ref[:stop])
        back_ref[span + start : span + stop] = back.astype(bf16)


def own_body(
    behind_logit_ref, own_logit_ref, own_win_ref, halo_ref, query_ref, key_ref, grad_ref,
    gq_ref, gk_ref, gv_ref,
):
    span = query_ref.shape[0]
    scale = 1.0 / math.sqrt(DH)
    for start in range(0, span, TILE):
        stop = start + TILE
        here = slice(start, stop)
        result = dot_tn(halo_ref[start:span], behind_logit_ref[start:, here])
        result = result + dot_tn(key_ref[:stop], own_logit_ref[:stop, here])
        gq_ref[here] = (jnp.transpose(result) * scale).astype(bf16)
        gk_ref[here] = dot_nn(own_logit_ref[here, start:], query_ref[start:]) * scale
        gv_ref[here] = dot_nn(own_win_ref[here, start:], grad_ref[start:])


def settle_body(gk_ref, gv_ref, back_ref, gk_out, gv_out, done_ref):
    span = gk_ref.shape[0]
    gk_out[...] = (gk_ref[...] + back_ref[:span].astype(f32)).astype(bf16)
    gv_out[...] = (gv_ref[...] + back_ref[span:].astype(f32)).astype(bf16)
    done_ref[...] = jnp.zeros_like(done_ref)


def local(
    query_lin, key_lin, value_lin, norm_gain, grad_normed, query_win, key_win, value_win, grad_win
):
    tokens, width = query_lin.shape
    blocks, heads = lax.axis_size("ctx"), lax.axis_size("head")
    rows = blocks // ROW
    my_index = lax.axis_index("ctx")
    where = my_index.astype(jnp.int32).reshape(1)
    row_groups = [[row * ROW + col for col in range(ROW)] for row in range(rows)]
    col_groups = [[row * ROW + col for row in range(rows)] for col in range(ROW)]
    gain = norm_gain.reshape(1, width)
    state = (DH, DH)
    block = (tokens, width)
    macs = tokens * DH * DH
    square = tokens * tokens * DH
    size = tokens * DH * 2
    in_vmem = pl.BlockSpec(memory_space=pltpu.VMEM)
    in_hbm = pl.BlockSpec(memory_space=pltpu.HBM)
    anywhere = pl.BlockSpec(memory_space=pl.ANY)
    copies = pltpu.SemaphoreType.DMA((ROW,))
    spreading = (pltpu.VMEM(state, bf16), pltpu.SemaphoreType.DMA((max(rows, ROW),)))

    def along_row(value):
        return lax.all_to_all(value, "ctx", 0, 0, axis_index_groups=row_groups)

    def along_col(value):
        return lax.all_to_all(value, "ctx", 0, 0, axis_index_groups=col_groups)

    def row_total(parts, flops, *ahead):
        return kernel_call(
            total_body,
            shaped((rows,) + state, bf16),
            flops,
            16 * DH * DH * 2,
            scratch=spreading,
            specs=[in_vmem] + [anywhere] * len(ahead),
            out_specs=in_hbm,
            ahead=len(ahead),
        )(parts, *ahead)

    def shift(value, steps):
        first, last = max(0, -steps), min(blocks, blocks - steps)
        return lax.ppermute(value, "ctx", [(at, at + steps) for at in range(first, last)])

    chosen = kernel_call(
        chosen_body,
        shaped((5 * ROW, TILE), f32),
        LONG,
        0,
        specs=[pl.BlockSpec(memory_space=pltpu.SMEM)],
    )(where)
    own_state = kernel_call(
        state_body,
        shaped((ROW,) + state, bf16),
        2 * macs,
        2 * size + ROW * DH * DH * 2,
        specs=[in_vmem] * 2 + [anywhere],
        ahead=1,
    )(key_lin, value_lin, chosen)
    parts = along_row(own_state)
    row_sum = row_total(parts, 8 * DH * DH)
    halo_pack = kernel_call(
        pack_body,
        shaped((2 * tokens, width), bf16),
        0,
        4 * size,
        specs=[in_vmem] * 2 + [anywhere],
        ahead=1,
    )(key_win, value_win, row_sum)
    halo = shift(halo_pack, 1)
    turned = (width, tokens)
    probs, kept, inner, scaled, base = kernel_call(
        inner_body,
        (
            shaped((tokens, tokens), bf16),
            shaped((2 * tokens, width), bf16),
            shaped(turned, f32),
            shaped(turned, f32),
            shaped(state, f32),
        ),
        2.5 * square,
        8 * size,
        specs=[in_vmem] * 7 + [anywhere],
        ahead=1,
    )(chosen, parts, query_lin, key_lin, value_lin, grad_normed, gain, row_sum)
    row_parts = along_col(row_sum)
    lin_out, prior, sums = kernel_call(
        normed_body,
        (shaped(turned, f32), shaped(state, f32), shaped((heads, 8, TILE), f32)),
        4 * macs,
        8 * size,
        scratch=(pltpu.VMEM((8, TILE), f32), pltpu.SemaphoreType.DMA((heads,))),
        specs=[in_vmem] + [in_vmem] * 5,
        out_specs=(in_vmem, in_vmem, in_hbm),
    )(chosen, row_parts, base, inner, query_lin, scaled)
    flat = shaped((tokens, tokens), bf16)
    back, behind_logit, own_logit, own_win = kernel_call(
        window_body,
        (shaped((2 * tokens, width), bf16), flat, flat, flat),
        8 * square,
        20 * size,
        tokens * tokens,
        (pltpu.VMEM((tokens, tokens), bf16),),
        16,
        [in_vmem] + [in_vmem] * 5 + [anywhere],
        ahead=1,
    )(chosen, query_win, key_win, value_win, grad_win, halo, sums)
    gq_win, gk_own, gv_own = kernel_call(
        own_body,
        (shaped(block, bf16), shaped(block, f32), shaped(block, f32)),
        LONG,
        20 * size,
        specs=[in_vmem] * 7 + [anywhere],
        ahead=1,
    )(behind_logit, own_logit, own_win, halo, query_win, key_win, grad_win, sums)
    all_sums = lax.all_to_all(sums, "head", 0, 0)
    returned = shift(back, -1)
    grad_out, later_state = kernel_call(
        functools.partial(grad_out_body, width=float(width * heads)),
        (shaped(turned, bf16), shaped((ROW,) + state, bf16)),
        2 * macs,
        8 * size,
        specs=[in_vmem] * 4 + [anywhere] * 2,
        ahead=2,
    )(all_sums, lin_out, scaled, query_lin, returned, gk_own)
    later_parts = along_row(later_state)
    later_sum = row_total(later_parts, 8 * DH * DH)
    gq_lin, gk_part, gv_part, later_base = kernel_call(
        mixed_body,
        (shaped(block, bf16), shaped(block, f32), shaped(block, f32), shaped(state, f32)),
        5 * square,
        10 * size,
        scratch=(pltpu.VMEM(block, bf16),),
        specs=[in_vmem] * 7 + [anywhere],
        ahead=1,
    )(chosen, later_parts, grad_out, query_lin, kept, probs, prior, later_sum)
    later_rows = along_col(later_sum)
    gk_win, gv_win, settled = kernel_call(
        settle_body,
        (shaped(block, bf16), shaped(block, bf16), shaped((8, TILE), f32)),
        tokens * DH,
        8 * size,
        specs=[in_vmem] * 3 + [anywhere],
        ahead=1,
    )(gk_own, gv_own, returned, later_sum)
    gk_lin, gv_lin = kernel_call(
        closing_body,
        (shaped(block, bf16),) * 2,
        8 * macs,
        8 * size,
        scratch=(pltpu.VMEM(block, bf16), pltpu.VMEM(block, bf16), copies),
        specs=[in_vmem] + [in_vmem] * 5 + [anywhere],
        out_specs=(in_hbm, in_hbm),
        ahead=1,
    )(chosen, later_rows, later_base, gk_part, gv_part, kept, settled)
    return gq_lin, gk_lin, gv_lin, gq_win, gk_win, gv_win


def solution(mesh):
    placed = P("ctx", "head")
    return jax.shard_map(
        local,
        mesh=mesh,
        in_specs=(placed, placed, placed, P("head")) + (placed,) * 5,
        out_specs=(placed,) * 6,
        check_vma=False,
    )
```
